32 devices in a mesh: dp: 8 (over z, y), tensor: 4 (over x, core).
Axes of the slice: x: 2, y: 2, z: 4, core: 2. Of those that a mesh axis runs over, the one named last changes fastest.
Arguments:
- attn_heads: bfloat16 [1024, 8192], P('dp', 'tensor'), may hold values from -6 to 6
- residual: bfloat16 [1024, 8192], P('dp', 'tensor'), may hold values from -6 to 6
- low_hidden: bfloat16 [1024, 8192], P('dp', 'tensor'), may hold values from -6 to 6
- mid_hidden: bfloat16 [1024, 8192], P('dp', 'tensor'), may hold values from -6 to 6
- out_weight: bfloat16 [8192, 8192], P('tensor', 'dp'), may hold values from -0.0625 to 0.0625
- join_weight: bfloat16 [3, 8192, 8192], P(None, 'tensor', 'dp'), may hold values from -0.0390625 to 0.0390625
- join_gain: float32 [8192], replicated, may hold values from 0.1 to 1.9
Outputs:
- joined_state: bfloat16 [1024, 8192], P(('dp', 'tensor'))
The draws below stay inside these ranges and needn't reach their ends.
All inputs are finite; a program needn't handle non-finite values.
Results may differ from the reference program's by a relative error of at most 0.0039.
Values may be sent and summed in bfloat16 or wider, within the bound.
No kernel may reach another device: no remote copies, remote signals or barrier semaphores. Data moves between devices by JAX's collectives and lax.ppermute only.
A program may use at most 128 MiB of HBM per device.

```python
import jax
import jax.numpy as jnp
from jax import lax

D = 8192
TOKENS = 1024


def steps_of(rng, dims, split, least, high):
    factor_of = 1.0
    for dim, blocks in split:
        heights = jax.random.uniform(jax.random.fold_in(jax.random.fold_in(rng, 6), dim), (blocks,), jnp.float32, least / len(split), high / len(split))
        factor_of = factor_of * jnp.repeat(jnp.exp(heights), dims[dim] // blocks).reshape((-1,) + (1,) * (len(dims) - 1 - dim))
    return factor_of


def normal_values(stream_key, shape, spread, reach, shards=(), held_as=jnp.bfloat16):
    level = steps_of(stream_key, shape, shards, -0.22, 0.18) if shards else 1.0
    entries = jax.random.normal(stream_key, shape, jnp.float32) * spread * level
    return jnp.minimum(jnp.maximum(entries, -reach), reach).astype(held_as)


def setup_inputs(seed: int = 0) -> dict:
    seeds = jax.random.split(jax.random.key(seed), 8)
    attn_heads = normal_values(seeds[0], (TOKENS, D), 1.0, 6.0, ((0, 8), (1, 4)))
    residual = normal_values(seeds[1], (TOKENS, D), 1.0, 6.0, ((0, 8), (1, 4)))
    low_hidden = normal_values(seeds[2], (TOKENS, D), 1.0, 6.0, ((0, 8), (1, 4)))
    mid_hidden = normal_values(seeds[3], (TOKENS, D), 1.0, 6.0, ((0, 8), (1, 4)))
    out_weight = normal_values(seeds[4], (D, D), D ** -0.5, 0.0625, ((0, 4), (1, 8)))
    join_weight = normal_values(seeds[5], (3, D, D), (3 * D) ** -0.5, 0.0390625, ((1, 4), (2, 8)))
    join_gain = jnp.clip(1.0 + 0.18 * jax.random.normal(seeds[6], (D,), jnp.float32), 0.1, 1.9)
    return {"attn_heads": attn_heads, "residual": residual, "low_hidden": low_hidden, "mid_hidden": mid_hidden, "out_weight": out_weight, "join_weight": join_weight, "join_gain": join_gain}


def reference(attn_heads, residual, low_hidden, mid_hidden, out_weight, join_weight, join_gain):
    head_sum = jnp.dot(attn_heads, out_weight, preferred_element_type=jnp.float32)
    top_hidden = (residual.astype(jnp.float32) + head_sum).astype(jnp.bfloat16)
    joined_sum = jnp.dot(low_hidden, join_weight[0], preferred_element_type=jnp.float32)
    joined_sum = joined_sum + jnp.dot(mid_hidden, join_weight[1], preferred_element_type=jnp.float32)
    joined_sum = joined_sum + jnp.dot(top_hidden, join_weight[2], preferred_element_type=jnp.float32)
    inverse_rms = lax.rsqrt(lax.optimization_barrier(jnp.mean(joined_sum * joined_sum, axis=1, keepdims=True)) + 1e-05)
    return (joined_sum * inverse_rms * join_gain.astype(jnp.float32)).astype(jnp.bfloat16)
```

```python
import jax
import jax.numpy as jnp
import numpy as np
from jax import lax
from jax.sharding import PartitionSpec as P


def ring_of(groups):
    half = groups // 2
    return [2 * q for q in range(half)] + [2 * q + 1 for q in reversed(range(half))]


def ring_gather(forward, backward):
    ring = ring_of(lax.axis_size("dp"))
    count = len(ring)
    up = [(ring[q], ring[(q + 1) % count]) for q in range(count)]
    down = [(target, source) for source, target in up]
    above, below = [forward], [backward]
    for _ in range(count - 1):
        above.append(lax.ppermute(above[-1], "dp", up))
        below.append(lax.ppermute(below[-1], "dp", down))
    return above, below


def swap(values, bit):
    return lax.ppermute(values, "tensor", [(t, t ^ bit) for t in range(lax.axis_size("tensor"))])


def pick(values, index, axis=0):
    return lax.dynamic_index_in_dim(values, index, axis, keepdims=False)


def reduce_over_x(pieces, x):
    while pieces.shape[0] > 1:
        half = pieces.shape[0] // 2
        pieces = pieces.reshape((2, half) + pieces.shape[1:])
        side = lax.rem(lax.div(x, half), 2)
        sent = pick(pieces, 1 - side).astype(jnp.bfloat16)
        pieces = pick(pieces, side) + swap(sent, 2 * half).astype(jnp.float32)
    return pieces[0]


def local(attn_heads, residual, low_hidden, mid_hidden, out_weight, join_weight, join_gain):
    groups, owners = lax.axis_size("dp"), lax.axis_size("tensor")
    tokens, features = attn_heads.shape
    width = out_weight.shape[1]
    xs = owners // 2
    side_rows = tokens // 2
    rows = tokens // owners
    per_owner = groups // owners
    rounds = 2 * per_owner

    ring = np.array(ring_of(groups))
    place_of = np.argsort(ring)
    dp, tensor = lax.axis_index("dp"), lax.axis_index("tensor")
    x, core = lax.div(tensor, 2), lax.rem(tensor, 2)
    place = jnp.asarray(place_of, jnp.int32)[dp]

    def sides(values):
        split = values.reshape((xs, 2, rows) + values.shape[1:])
        return [split[:, s].reshape((side_rows,) + values.shape[1:]) for s in range(2)]

    def slot_of(q):
        return jnp.where(core == 0, lax.rem(place - q + groups, groups), lax.rem(q - place + groups, groups))

    attn_up, attn_down = ring_gather(*sides(attn_heads))
    low_sides, mid_sides = sides(low_hidden), sides(mid_hidden)
    depth_sides = [jnp.stack([low_sides[s], mid_sides[s]]) for s in range(2)]
    depth_sides[0], depth_sides[1], last_up, last_down = lax.optimization_barrier(
        (depth_sides[0], depth_sides[1], attn_up[-1], attn_down[-1])
    )
    attn_up[-1], attn_down[-1] = last_up, last_down
    depth_up, depth_down = ring_gather(*depth_sides)

    attn_all = jnp.concatenate(attn_up + attn_down, axis=0)
    head_partial = jnp.dot(attn_all, out_weight, preferred_element_type=jnp.float32)
    head_partial = head_partial.reshape(2, groups, side_rows, width)
    head_core = pick(head_partial, core) + swap(pick(head_partial, 1 - core), 1)
    by_place = jnp.stack([pick(head_core, slot_of(q)) for q in range(groups)])
    held = reduce_over_x(by_place.reshape(xs, rounds, side_rows, width), x).astype(jnp.bfloat16)

    shift = 2 * lax.rem(dp, per_owner) + core
    arrived = []
    for k in range(rounds):
        moves = []
        for d in range(groups):
            for t in range(owners):
                q = (t // 2) * rounds + (k - 2 * (d % per_owner) - t % 2) % rounds
                moves.append((d * owners + t, int(ring[q]) * owners + d // per_owner))
        piece = pick(held, lax.rem(k - shift + 2 * rounds, rounds))
        arrived.append(lax.ppermute(piece, ("dp", "tensor"), moves))
    arrived = jnp.stack(arrived)
    top_sides = []
    for s, rest in enumerate(sides(residual)):
        blocks = [pick(arrived, lax.rem(place + 2 * j + s, rounds)) for j in range(per_owner)]
        head_sum = jnp.concatenate(blocks, axis=1).astype(jnp.float32)
        top_sides.append((rest.astype(jnp.float32) + head_sum).astype(jnp.bfloat16))
    top_up, top_down = ring_gather(*top_sides)

    depth_all = jnp.concatenate(depth_up + depth_down, axis=1)
    top_all = jnp.concatenate(top_up + top_down, axis=0)
    joined = jnp.dot(depth_all[0], join_weight[0], preferred_element_type=jnp.float32)
    joined = joined + jnp.dot(depth_all[1], join_weight[1], preferred_element_type=jnp.float32)
    joined = joined + jnp.dot(top_all, join_weight[2], preferred_element_type=jnp.float32)
    joined = joined.reshape(2, groups, side_rows, width)
    joined_core = pick(joined, core) + swap(pick(joined, 1 - core), 1)
    by_owner = jnp.moveaxis(joined_core.reshape(groups, xs, rows, width), 1, 0)
    owned = reduce_over_x(by_owner, x)
    by_group = jnp.stack([pick(owned, slot_of(int(place_of[g]))) for g in range(groups)]).astype(jnp.bfloat16)
    moved = lax.all_to_all(by_group, "dp", split_axis=0, concat_axis=0, tiled=True)
    joined_sum = jnp.moveaxis(moved, 0, 1).reshape(rows, groups * width).astype(jnp.float32)
    inverse_rms = lax.rsqrt(jnp.mean(joined_sum * joined_sum, axis=1, keepdims=True) + 1e-05)
    return (joined_sum * inverse_rms * join_gain).astype(jnp.bfloat16)


def solution(mesh):
    return jax.shard_map(
        local,
        mesh=mesh,
        in_specs=(
            P("dp", "tensor"),
            P("dp", "tensor"),
            P("dp", "tensor"),
            P("dp", "tensor"),
            P("tensor", "dp"),
            P(None, "tensor", "dp"),
            P(),
        ),
        out_specs=P(("dp", "tensor"), None),
        check_vma=False,
    )
```

```python
import jax
import jax.numpy as jnp
import numpy as np
from jax import lax
from jax.sharding import PartitionSpec as P


def ring_of(groups):
    half = groups // 2
    return [2 * q for q in range(half)] + [2 * q + 1 for q in reversed(range(half))]


def ring_gather(forward, backward):
    ring = ring_of(lax.axis_size("dp"))
    count = len(ring)
    up = [(ring[q], ring[(q + 1) % count]) for q in range(count)]
    down = [(target, source) for source, target in up]
    above, below = [forward], [backward]
    for _ in range(count - 1):
        above.append(lax.ppermute(above[-1], "dp", up))
        below.append(lax.ppermute(below[-1], "dp", down))
    return above, below


def swap(values, bit):
    return lax.ppermute(values, "tensor", [(t, t ^ bit) for t in range(lax.axis_size("tensor"))])


def pick(values, index, axis=0):
    return lax.dynamic_index_in_dim(values, index, axis, keepdims=False)


def reduce_over_x(pieces, x):
    while pieces.shape[0] > 1:
        half = pieces.shape[0] // 2
        pieces = pieces.reshape((2, half) + pieces.shape[1:])
        side = lax.rem(lax.div(x, half), 2)
        sent = pick(pieces, 1 - side).astype(jnp.bfloat16)
        pieces = pick(pieces, side) + swap(sent, 2 * half).astype(jnp.float32)
    return pieces[0]


def local(attn_heads, residual, low_hidden, mid_hidden, out_weight, join_weight, join_gain):
    groups, owners = lax.axis_size("dp"), lax.axis_size("tensor")
    tokens, features = attn_heads.shape
    width = out_weight.shape[1]
    xs = owners // 2
    side_rows = tokens // 2
    rows = tokens // owners
    per_owner = groups // owners
    rounds = 2 * per_owner

    ring = np.array(ring_of(groups))
    place_of = np.argsort(ring)
    dp, tensor = lax.axis_index("dp"), lax.axis_index("tensor")
    x, core = lax.div(tensor, 2), lax.rem(tensor, 2)
    place = jnp.asarray(place_of, jnp.int32)[dp]

    def sides(values):
        split = values.reshape((xs, 2, rows) + values.shape[1:])
        return [split[:, s].reshape((side_rows,) + values.shape[1:]) for s in range(2)]

    def slot_of(q):
        return jnp.where(core == 0, lax.rem(place - q + groups, groups), lax.rem(q - place + groups, groups))

    depth_pair = jnp.concatenate(sides(jnp.concatenate([low_hidden, mid_hidden], axis=1)), axis=0)
    depth_all = lax.all_gather(depth_pair, "dp", axis=0, tiled=True)

    def both_sides(up, down, weight):
        product = jnp.dot(jnp.concatenate(up + down, axis=0), weight, preferred_element_type=jnp.float32)
        return product.reshape(2, len(up), side_rows, width)

    def sum_cores(products):
        return pick(products, core) + swap(pick(products, 1 - core), 1)

    attn_up, attn_down = ring_gather(*sides(attn_heads))
    head_core = jnp.concatenate(
        [
            sum_cores(both_sides(attn_up[low:high], attn_down[low:high], out_weight))
            for low, high in ((0, groups - 2), (groups - 2, groups))
        ]
    )
    by_place = jnp.stack([pick(head_core, slot_of(q)) for q in range(groups)])
    held = reduce_over_x(by_place.reshape(xs, rounds, side_rows, width), x).astype(jnp.bfloat16)

    shift = 2 * lax.rem(dp, per_owner) + core
    arrived = []
    for k in range(rounds):
        moves = []
        for d in range(groups):
            for t in range(owners):
                q = (t // 2) * rounds + (k - 2 * (d % per_owner) - t % 2) % rounds
                moves.append((d * owners + t, int(ring[q]) * owners + d // per_owner))
        piece = pick(held, lax.rem(k - shift + 2 * rounds, rounds))
        arrived.append(lax.ppermute(piece, ("dp", "tensor"), moves))
    arrived = jnp.stack(arrived)
    top_sides = []
    for s, rest in enumerate(sides(residual)):
        blocks = [pick(arrived, lax.rem(place + 2 * j + s, rounds)) for j in range(per_owner)]
        head_sum = jnp.concatenate(blocks, axis=1).astype(jnp.float32)
        top_sides.append((rest.astype(jnp.float32) + head_sum).astype(jnp.bfloat16))
    top_up, top_down = ring_gather(*top_sides)

    joined_depths = jnp.dot(depth_all, join_weight[:2].reshape(2 * features, width), preferred_element_type=jnp.float32)
    joined_depths = joined_depths.reshape(groups, 2, side_rows, width)
    ring_index = jnp.asarray(ring, jnp.int32)
    owned = []
    starts = sorted({0, groups // 2 - 1, groups - 3, groups - 1, groups})
    for low, high in zip(starts, starts[1:]):
        product = both_sides(top_up[low:high], top_down[low:high], join_weight[2])
        rest = [
            [pick(joined_depths, ring_index[lax.rem(place + sign * s + groups, groups)])[side] for s in range(low, high)]
            for side, sign in ((0, -1), (1, 1))
        ]
        joined_core = sum_cores(product + jnp.stack([jnp.stack(part) for part in rest]))
        by_owner = jnp.moveaxis(joined_core.reshape(high - low, xs, rows, width), 1, 0)
        chunk = reduce_over_x(by_owner, x).astype(jnp.bfloat16)
        for s in range(low, high):
            moves = [
                (int(ring[q]) * owners + t, int(ring[(q + (s if t % 2 else -s)) % groups]) * owners + t)
                for q in range(groups)
                for t in range(owners)
            ]
            owned.append(lax.ppermute(chunk[s - low], ("dp", "tensor"), moves) if s else chunk[0])
    owned = jnp.stack(owned)
    by_columns = []
    for g in range(groups):
        ahead = lax.rem(int(place_of[g]) - place + groups, groups)
        by_columns.append(pick(owned, jnp.where(core == 0, ahead, lax.rem(groups - ahead, groups))))
    joined_sum = jnp.concatenate(by_columns, axis=1).astype(jnp.float32)
    inverse_rms = lax.rsqrt(jnp.mean(joined_sum * joined_sum, axis=1, keepdims=True) + 1e-05)
    return (joined_sum * inverse_rms * join_gain).astype(jnp.bfloat16)


def solution(mesh):
    return jax.shard_map(
        local,
        mesh=mesh,
        in_specs=(
            P("dp", "tensor"),
            P("dp", "tensor"),
            P("dp", "tensor"),
            P("dp", "tensor"),
            P("tensor", "dp"),
            P(None, "tensor", "dp"),
            P(),
        ),
        out_specs=P(("dp", "tensor"), None),
        check_vma=False,
    )
```

```python
import functools

import jax
import jax.numpy as jnp
import numpy as np
from jax import lax
from jax.experimental import pallas as pl
from jax.experimental.pallas import tpu as pltpu
from jax.sharding import PartitionSpec as P


def ring_of(groups):
    half = groups // 2
    return [2 * q for q in range(half)] + [2 * q + 1 for q in reversed(range(half))]


def home_rounds(groups, owners):
    ring = ring_of(groups)
    xs, per_owner = owners // 2, groups // owners
    moves = {}
    for p, d in enumerate(ring):
        for t in range(owners):
            x, core = t // 2, t % 2
            for k in range(groups // xs):
                s = k * xs + x
                q = (p + (s if core else -s)) % groups
                moves.setdefault(d * owners + t, []).append((ring[q] * owners + d // per_owner, k, 2 * (d % per_owner) + core))
    pairs, items, pieces = [], [], []
    for _ in range(groups // xs):
        taken = {}

        def place(source, seen):
            for move in moves[source]:
                if move[0] not in seen:
                    seen.add(move[0])
                    if move[0] not in taken or place(taken[move[0]][0], seen):
                        taken[move[0]] = (source, move)
                        return True
            return False

        for source in sorted(moves):
            place(source, set())
        pairs.append(sorted((source, target) for target, (source, _) in taken.items()))
        items.append([0] * len(moves))
        pieces.append([0] * len(moves))
        for target, (source, move) in taken.items():
            items[-1][source] = move[1]
            pieces[-1][target] = move[2]
            moves[source].remove(move)
    return pairs, np.array(items, np.uint32).T, np.array(pieces, np.int32).T


def tie(values, after):
    flat, tree = jax.tree.flatten(values)
    held = lax.optimization_barrier(tuple(flat) + tuple(jax.tree.leaves(after)))
    return jax.tree.unflatten(tree, held[: len(flat)])


def pick(values, index):
    return lax.dynamic_index_in_dim(values, index, 0, keepdims=False)


def top_body(rounds, width, pieces_ref, *refs):
    arrived, rests, tops = refs[:rounds], refs[rounds : rounds + 2], refs[rounds + 2 :]
    for k in range(rounds):
        piece = pieces_ref[0, k]
        columns = pl.ds(pl.multiple_of(lax.div(piece, 2) * width, width), width)
        for side in range(2):

            @pl.when(lax.rem(piece, 2) == side)
            def _(side=side, k=k, columns=columns):
                total = rests[side][:, columns].astype(jnp.float32) + arrived[k][...].astype(jnp.float32)
                tops[side][:, columns] = total.astype(jnp.bfloat16)


def norm_body(groups, width, *refs):
    slots, gain_ref, out_ref = refs[:groups], refs[groups], refs[groups + 1]
    dp, core = lax.axis_index("dp"), lax.rem(lax.axis_index("tensor"), 2)
    place = jnp.where(lax.rem(dp, 2) == 0, lax.div(dp, 2), groups - 1 - lax.div(dp, 2))
    total = 0.0
    for slot in slots:
        block = slot[...].astype(jnp.float32)
        total = total + jnp.sum(block * block, axis=1, keepdims=True)
    inverse_rms = lax.rsqrt(total / (groups * width) + 1e-05)
    for s, slot in enumerate(slots):
        q = lax.rem(place + jnp.where(core == 0, s, groups - s), groups)
        d = jnp.where(q < groups // 2, 2 * q, 2 * (groups - 1 - q) + 1)
        columns = pl.ds(pl.multiple_of(d * width, width), width)
        out_ref[:, columns] = (slot[...].astype(jnp.float32) * inverse_rms * gain_ref[:, columns]).astype(jnp.bfloat16)


VMEM = pl.BlockSpec(memory_space=pltpu.VMEM)
SMEM = pl.BlockSpec(memory_space=pltpu.SMEM)


def local(attn_heads, residual, low_hidden, mid_hidden, out_weight, join_weight, join_gain):
    groups, owners = lax.axis_size("dp"), lax.axis_size("tensor")
    tokens, features = attn_heads.shape
    width = out_weight.shape[1]
    xs = owners // 2
    side_rows = tokens // 2
    rows = tokens // owners
    ring = ring_of(groups)
    up = [(ring[q], ring[(q + 1) % groups]) for q in range(groups)]
    down = [(target, source) for source, target in up]
    tensor = lax.axis_index("tensor").astype(jnp.uint32)
    core, x = tensor & 1, tensor >> 1
    device = lax.axis_index("dp").astype(jnp.uint32) * owners + tensor

    def sides(values):
        split = values.reshape((xs, 2, rows) + values.shape[1:])
        return [split[:, s].reshape((side_rows,) + values.shape[1:]) for s in range(2)]

    def hop(pair):
        return [lax.ppermute(pair[0], "dp", up), lax.ppermute(pair[1], "dp", down)]

    def swap(values, bit):
        return lax.ppermute(values, "tensor", [(t, t ^ bit) for t in range(owners)])

    def product(pairs, weight):
        rows_in = jnp.concatenate([pair[s] for s in range(2) for pair in pairs], axis=0)
        return jnp.dot(rows_in, weight, preferred_element_type=jnp.float32).reshape(2, len(pairs), side_rows, width)

    def sum_cores(products):
        return pick(products, core) + swap(pick(products, 1 - core), 1)

    def sum_xs(pieces):
        half = pieces.shape[0] // 2
        while half:
            pieces = pieces.reshape((2, half) + pieces.shape[1:])
            side = (x >> (half.bit_length() - 1)) & 1
            pieces = pick(pieces, side) + swap(pick(pieces, 1 - side), 2 * half)
            half //= 2
        return pieces[0]

    attn = [sides(attn_heads)]
    deep = [[jnp.stack(pair) for pair in zip(sides(low_hidden), sides(mid_hidden))]]
    heads = []
    cuts = sorted({0, groups // 2, groups - xs, groups})
    for step in range(1, groups):
        if step % 2:
            deep.append(hop(tie(deep[-1], attn[-1]) if step > 1 else deep[-1]))
        attn.append(hop(attn[-1]))
    deep.append(hop(tie(deep[-1], attn[-1])))
    for low, high in zip(cuts, cuts[1:]):
        summed = sum_cores(product(attn[low:high], out_weight))
        by_x = jnp.moveaxis(summed.reshape((high - low) // xs, xs, side_rows, width), 1, 0)
        heads.append((summed, sum_xs(by_x)))
    for after in heads[-1]:
        if len(deep) < groups:
            deep.append(hop(tie(deep[-1], after)))
    while len(deep) < groups:
        deep.append(hop(deep[-1]))
    held = jnp.concatenate([part for _, part in heads], axis=0).astype(jnp.bfloat16)

    pairs, items, pieces = home_rounds(groups, owners)
    item = lax.dynamic_slice(jnp.asarray(items), (device, jnp.uint32(0)), (1, len(pairs)))
    piece = lax.dynamic_slice(jnp.asarray(pieces), (device, jnp.uint32(0)), (1, len(pairs)))
    arrived = [lax.ppermute(pick(held, item[0, k]), ("dp", "tensor"), moves) for k, moves in enumerate(pairs)]
    side_shape = jax.ShapeDtypeStruct((side_rows, features), jnp.bfloat16)
    top = [
        pl.pallas_call(
            functools.partial(top_body, len(pairs), width),
            out_shape=[side_shape] * 2,
            in_specs=[SMEM] + [VMEM] * (len(pairs) + 2),
            out_specs=[VMEM] * 2,
            name="add_residual",
        )(piece, *arrived, *sides(residual))
    ]

    low_sum = product([[side[0] for side in pair] for pair in deep], join_weight[0])
    deep_sum = low_sum + product([[side[1] for side in pair] for pair in deep], join_weight[1])
    cuts = sorted({0, groups // 2 - 1, groups - 3, groups - 1, groups})
    chunks = []

    def start_chunk():
        low, high = cuts[len(chunks)], cuts[len(chunks) + 1]
        chunks.append([product(top[low:high], join_weight[2]) + deep_sum[:, low:high]])

    def step_chunk(chunk):
        if len(chunk) == 1:
            chunk.append(sum_cores(chunk[0]))
        elif len(chunk) == 2:
            by_owner = chunk[1].reshape(chunk[1].shape[0], xs, rows, width)
            chunk.append(sum_xs(jnp.moveaxis(by_owner, 1, 0)))

    for step in range(1, groups):
        pair = top[-1]
        if step == 2:
            pair = tie(pair, low_sum)
        elif step == 3:
            pair = tie(pair, deep_sum)
        elif chunks:
            pair = tie(pair, [chunk[-1] for chunk in chunks])
        top.append(hop(pair))
        for chunk in chunks:
            step_chunk(chunk)
        if step == cuts[len(chunks) + 1]:
            start_chunk()
    while len(chunks) < len(cuts) - 1:
        start_chunk()
    for chunk in chunks:
        while len(chunk) < 3:
            step_chunk(chunk)

    owned = [part for chunk in chunks for part in chunk[-1]]
    for s in range(1, groups):
        moves = [
            (ring[q] * owners + t, ring[(q + (s if t % 2 else -s)) % groups] * owners + t)
            for q in range(groups)
            for t in range(owners)
        ]
        owned[s] = lax.ppermute(owned[s].astype(jnp.bfloat16), ("dp", "tensor"), moves)
    return pl.pallas_call(
        functools.partial(norm_body, groups, width),
        out_shape=jax.ShapeDtypeStruct((rows, groups * width), jnp.bfloat16),
        in_specs=[VMEM] * (groups + 1),
        out_specs=VMEM,
        name="norm_rows",
    )(*owned, join_gain.reshape(1, groups * width))


def solution(mesh):
    return jax.shard_map(
        local,
        mesh=mesh,
        in_specs=(
            P("dp", "tensor"),
            P("dp", "tensor"),
            P("dp", "tensor"),
            P("dp", "tensor"),
            P("tensor", "dp"),
            P(None, "tensor", "dp"),
            P(),
        ),
        out_specs=P(("dp", "tensor"), None),
        check_vma=False,
    )
```

```python
import functools

import jax
import jax.numpy as jnp
from jax import lax
from jax.experimental import pallas as pl
from jax.experimental.pallas import tpu as pltpu
from jax.sharding import PartitionSpec as P


def ring_of(groups):
    half = groups // 2
    return [2 * q for q in range(half)] + [2 * q + 1 for q in reversed(range(half))]


def tie(values, after):
    flat, tree = jax.tree.flatten(values)
    held = lax.optimization_barrier(tuple(flat) + tuple(jax.tree.leaves(after)))
    return jax.tree.unflatten(tree, held[: len(flat)])


def pick(values, index):
    return lax.dynamic_index_in_dim(values, index, 0, keepdims=False)


def place_on_ring(groups):
    dp = lax.axis_index("dp")
    return jnp.where(lax.rem(dp, 2) == 0, lax.div(dp, 2), groups - 1 - lax.div(dp, 2))


def top_body(groups, classes, width, *refs):
    arrived, rest_ref, top_ref = refs[: len(classes)], refs[-2], refs[-1]
    home = lax.axis_index("tensor") + place_on_ring(groups)
    for kind, piece_ref in zip(classes, arrived):
        j = lax.rem(home + kind, len(classes))
        columns = pl.ds(pl.multiple_of(j * width, width), width)
        total = rest_ref[:, columns].astype(jnp.float32) + piece_ref[...].astype(jnp.float32)
        top_ref[:, columns] = total.astype(jnp.bfloat16)


def norm_body(offsets, width, *refs):
    groups = len(offsets)
    slots, gain_ref, out_ref = refs[:groups], refs[groups], refs[groups + 1]
    place = place_on_ring(groups)
    total = 0.0
    for slot in slots:
        block = slot[...].astype(jnp.float32)
        total = total + jnp.sum(block * block, axis=1, keepdims=True)
    inverse_rms = lax.rsqrt(total / (groups * width) + 1e-05)
    for offset, slot in zip(offsets, slots):
        q = lax.rem(place + offset + groups, groups)
        d = jnp.where(q < groups // 2, 2 * q, 2 * (groups - 1 - q) + 1)
        columns = pl.ds(pl.multiple_of(d * width, width), width)
        out_ref[:, columns] = (slot[...].astype(jnp.float32) * inverse_rms * gain_ref[:, columns]).astype(jnp.bfloat16)


VMEM = pl.BlockSpec(memory_space=pltpu.VMEM)


class Gather:
    def __init__(self, own, axis):
        self.ring = ring_of(lax.axis_size("dp"))
        self.axis, self.last, self.hops = axis, len(self.ring) // 2, 0
        self.ends = [own, own]
        self.slots = {0: [own]}

    def hop(self, after=()):
        count = len(self.ring)
        ends = tie(self.ends, after) if jax.tree.leaves(after) else self.ends
        self.hops += 1
        if self.hops == self.last:
            middle = ends[0].shape[self.axis] // 2
            ends = [
                lax.slice_in_dim(ends[0], 0, middle, axis=self.axis),
                lax.slice_in_dim(ends[1], middle, 2 * middle, axis=self.axis),
            ]
        up = [(self.ring[q], self.ring[(q + 1) % count]) for q in range(count)]
        down = [(target, source) for source, target in up]
        self.ends = [lax.ppermute(ends[0], "dp", up), lax.ppermute(ends[1], "dp", down)]
        if self.hops == self.last:
            self.slots[self.hops] = self.ends
        else:
            self.slots[self.hops], self.slots[-self.hops] = [self.ends[0]], [self.ends[1]]


def local(attn_heads, residual, low_hidden, mid_hidden, out_weight, join_weight, join_gain):
    groups, owners = lax.axis_size("dp"), lax.axis_size("tensor")
    tokens, features = attn_heads.shape
    width = out_weight.shape[1]
    xs = owners // 2
    rows = tokens // owners
    ring = ring_of(groups)
    last = groups // 2
    offsets = [0] + [sign * s for s in range(1, last) for sign in (1, -1)] + [last]
    tensor = lax.axis_index("tensor").astype(jnp.uint32)
    core, x = tensor & 1, tensor >> 1

    def swap(values, bit):
        return lax.ppermute(values, "tensor", [(t, t ^ bit) for t in range(owners)])

    def product(slots, weight):
        rows_in = jnp.concatenate([piece for slot in slots for piece in slot], axis=0)
        return jnp.dot(rows_in, weight, preferred_element_type=jnp.float32).reshape(len(slots), tokens, width)

    def bit_of_x(half):
        return (x >> (half.bit_length() - 1)) & 1

    attn = Gather(attn_heads, 0)
    per_owner = groups // owners
    classes = list(reversed(range(per_owner)))
    kept = {kind: [k for k in offsets if k % per_owner == kind] for kind in classes}
    pair_sums = {kind: [] for kind in classes}

    def sum_pairs():
        for kind in classes:
            while len(pair_sums[kind]) < xs:
                i = 2 * len(pair_sums[kind])
                pair = kept[kind][i : i + 2]
                if not all(k in attn.slots for k in pair):
                    break
                products = product([attn.slots[k] for k in pair], out_weight)
                pair_sums[kind].append(pick(products, core) + swap(pick(products, 1 - core), 1))

    while attn.hops < last:
        ready = [pair_sums[kind] for kind in classes]
        ready = [list(part) for part in ready]
        if attn.hops:
            sum_pairs()
        attn.hop(ready)
    arrived_heads = attn.ends
    sum_pairs()

    def sum_xs(parts):
        while len(parts) > 1:
            half = len(parts) // 2
            high = bit_of_x(half) == 1
            sent = jnp.stack([jnp.where(high, a, b) for a, b in zip(parts[:half], parts[half:])]).astype(jnp.bfloat16)
            came = swap(sent, 2 * half)
            parts = [
                jnp.where(high, b, a) + came[i].astype(jnp.float32)
                for i, (a, b) in enumerate(zip(parts[:half], parts[half:]))
            ]
        return parts[0]

    arrived = []
    for kind in classes:
        held = sum_xs(pair_sums[kind]).astype(jnp.bfloat16)
        moves = [
            (d * owners + t, ring[(p - kept[kind][t]) % groups] * owners + d // per_owner)
            for p, d in enumerate(ring)
            for t in range(owners)
        ]
        arrived.append(lax.ppermute(held, ("dp", "tensor"), moves))
    own_top = pl.pallas_call(
        functools.partial(top_body, groups, classes, width),
        out_shape=jax.ShapeDtypeStruct((tokens, features), jnp.bfloat16),
        in_specs=[VMEM] * (len(classes) + 1),
        out_specs=VMEM,
        name="add_residual",
    )(*arrived, residual)

    deep = Gather(jnp.stack([low_hidden, mid_hidden]), 1)
    deep.hop(arrived_heads)
    deep.hop(held)
    top = Gather(own_top, 0)
    cuts = [0] + list(range(3, groups, 2)) + [groups]
    chunks = []

    def start_chunk():
        part = offsets[cuts[len(chunks)] : cuts[len(chunks) + 1]]
        total = product([top.slots[k] for k in part], join_weight[2])
        for depth in range(2):
            total = total + product([[piece[depth] for piece in deep.slots[k]] for k in part], join_weight[depth])
        chunks.append([total])

    def step_chunk(chunk):
        if len(chunk) == 1:
            by_owner = chunk[0].reshape(chunk[0].shape[0], xs, 2, rows, width)
            kept_part = lax.dynamic_index_in_dim(by_owner, core, 2, keepdims=False)
            sent_part = lax.dynamic_index_in_dim(by_owner, 1 - core, 2, keepdims=False)
            chunk.append(kept_part + swap(sent_part, 1))
        elif len(chunk) == 2:
            part, half = chunk[1], xs // 2
            while half:
                part = part.reshape((part.shape[0], 2, half) + part.shape[-2:])
                side = bit_of_x(half)
                part = lax.dynamic_index_in_dim(part, side, 1, keepdims=False) + swap(
                    lax.dynamic_index_in_dim(part, 1 - side, 1, keepdims=False), 2 * half
                )
                half //= 2
            chunk.append(part.reshape(part.shape[0], rows, width))

    while top.hops < last:
        top.hop([chunk[-1] for chunk in chunks])
        if deep.hops < last:
            deep.hop(top.ends)
        for chunk in chunks:
            step_chunk(chunk)
        if top.hops > 1:
            start_chunk()
            step_chunk(chunks[-1])
    while len(chunks) < len(cuts) - 1:
        start_chunk()
    for chunk in chunks:
        while len(chunk) < 3:
            step_chunk(chunk)

    owned = [part for chunk in chunks for part in chunk[-1]]
    for i, k in enumerate(offsets):
        if k:
            moves = [(ring[q], ring[(q - k) % groups]) for q in range(groups)]
            owned[i] = lax.ppermute(owned[i].astype(jnp.bfloat16), "dp", moves)
    return pl.pallas_call(
        functools.partial(norm_body, offsets, width),
        out_shape=jax.ShapeDtypeStruct((rows, groups * width), jnp.bfloat16),
        in_specs=[VMEM] * (groups + 1),
        out_specs=VMEM,
        name="norm_rows",
    )(*owned, join_gain.reshape(1, groups * width))


def solution(mesh):
    return jax.shard_map(
        local,
        mesh=mesh,
        in_specs=(
            P("dp", "tensor"),
            P("dp", "tensor"),
            P("dp", "tensor"),
            P("dp", "tensor"),
            P("tensor", "dp"),
            P(None, "tensor", "dp"),
            P(),
        ),
        out_specs=P(("dp", "tensor"), None),
        check_vma=False,
    )
```

```python
import functools

import jax
import jax.numpy as jnp
import numpy as np
from jax import lax
from jax.experimental import pallas as pl
from jax.experimental.pallas import tpu as pltpu
from jax.sharding import PartitionSpec as P


def ring_of(groups):
    half = groups // 2
    return [2 * q for q in range(half)] + [2 * q + 1 for q in reversed(range(half))]


def tie(values, after):
    flat, tree = jax.tree.flatten(values)
    held = lax.optimization_barrier(tuple(flat) + tuple(jax.tree.leaves(after)))
    return jax.tree.unflatten(tree, held[: len(flat)])


def pick(values, index):
    return lax.dynamic_index_in_dim(values, index, 0, keepdims=False)


def place_on_ring(groups):
    dp = lax.axis_index("dp")
    return jnp.where(lax.rem(dp, 2) == 0, lax.div(dp, 2), groups - 1 - lax.div(dp, 2))


def top_body(groups, classes, width, *refs):
    arrived, rest_ref, top_ref = refs[: len(classes)], refs[-2], refs[-1]
    home = lax.axis_index("tensor") + place_on_ring(groups)
    for kind, piece_ref in zip(classes, arrived):
        j = lax.rem(home + kind, len(classes))
        columns = pl.ds(pl.multiple_of(j * width, width), width)
        total = rest_ref[:, columns].astype(jnp.float32) + piece_ref[...].astype(jnp.float32)
        top_ref[:, columns] = total.astype(jnp.bfloat16)


def norm_body(offsets, width, *refs):
    groups = len(offsets)
    slots, gain_ref, out_ref = refs[:groups], refs[groups], refs[groups + 1]
    place = place_on_ring(groups)
    total = 0.0
    for slot in slots:
        block = slot[...].astype(jnp.float32)
        total = total + jnp.sum(block * block, axis=1, keepdims=True)
    inverse_rms = lax.rsqrt(total / (groups * width) + 1e-05)
    for offset, slot in zip(offsets, slots):
        q = lax.rem(place + offset + groups, groups)
        d = jnp.where(q < groups // 2, 2 * q, 2 * (groups - 1 - q) + 1)
        columns = pl.ds(pl.multiple_of(d * width, width), width)
        out_ref[:, columns] = (slot[...].astype(jnp.float32) * inverse_rms * gain_ref[:, columns]).astype(jnp.bfloat16)


VMEM = pl.BlockSpec(memory_space=pltpu.VMEM)


class Gather:
    def __init__(self, own, axis):
        self.ring = ring_of(lax.axis_size("dp"))
        self.axis, self.last, self.hops = axis, len(self.ring) // 2, 0
        self.ends = [own, own]
        self.slots = {0: [own]}

    def hop(self, after=()):
        count = len(self.ring)
        ends = tie(self.ends, after) if jax.tree.leaves(after) else self.ends
        self.hops += 1
        if self.hops == self.last:
            middle = ends[0].shape[self.axis] // 2
            ends = [
                lax.slice_in_dim(ends[0], 0, middle, axis=self.axis),
                lax.slice_in_dim(ends[1], middle, 2 * middle, axis=self.axis),
            ]
        up = [(self.ring[q], self.ring[(q + 1) % count]) for q in range(count)]
        down = [(target, source) for source, target in up]
        self.ends = [lax.ppermute(ends[0], "dp", up), lax.ppermute(ends[1], "dp", down)]
        if self.hops == self.last:
            self.slots[self.hops] = self.ends
        else:
            self.slots[self.hops], self.slots[-self.hops] = [self.ends[0]], [self.ends[1]]


def local(attn_heads, residual, low_hidden, mid_hidden, out_weight, join_weight, join_gain):
    groups, owners = lax.axis_size("dp"), lax.axis_size("tensor")
    tokens, features = attn_heads.shape
    width = out_weight.shape[1]
    xs = owners // 2
    rows = tokens // owners
    ring = ring_of(groups)
    last = groups // 2
    offsets = [0] + [sign * s for s in range(1, last) for sign in (1, -1)] + [last]
    tensor = lax.axis_index("tensor").astype(jnp.uint32)
    core, x = tensor & 1, tensor >> 1

    def swap(values, bit):
        return lax.ppermute(values, "tensor", [(t, t ^ bit) for t in range(owners)])

    def product(slots, weight):
        rows_in = jnp.concatenate([piece for slot in slots for piece in slot], axis=0)
        return jnp.dot(rows_in, weight, preferred_element_type=jnp.float32).reshape(len(slots), tokens, width)

    def bit_of_x(half):
        return (x >> (half.bit_length() - 1)) & 1

    low_all = lax.all_gather(low_hidden, "dp", axis=0, tiled=True)
    group_table = np.array([[ring[(p - k) % groups] for k in offsets] for p in np.argsort(ring)], np.uint32)
    group_at = lax.dynamic_slice(
        jnp.asarray(group_table), (lax.axis_index("dp").astype(jnp.uint32), jnp.uint32(0)), (1, groups)
    )

    attn = Gather(attn_heads, 0)
    per_owner = groups // owners
    classes = list(reversed(range(per_owner)))
    kept = {kind: [k for k in offsets if k % per_owner == kind] for kind in classes}
    pair_sums = {kind: [] for kind in classes}

    def sum_pairs():
        for kind in classes:
            while len(pair_sums[kind]) < xs:
                i = 2 * len(pair_sums[kind])
                pair = kept[kind][i : i + 2]
                if not all(k in attn.slots for k in pair):
                    break
                products = product([attn.slots[k] for k in pair], out_weight)
                pair_sums[kind].append(pick(products, core) + swap(pick(products, 1 - core), 1))

    while attn.hops < last:
        ready = [pair_sums[kind] for kind in classes]
        ready = [list(part) for part in ready]
        if attn.hops:
            sum_pairs()
        attn.hop(ready)
    mid_all = lax.all_gather(tie(mid_hidden, attn.ends), "dp", axis=0, tiled=True)
    sum_pairs()

    def sum_xs(parts):
        while len(parts) > 1:
            half = len(parts) // 2
            high = bit_of_x(half) == 1
            sent = jnp.stack([jnp.where(high, a, b) for a, b in zip(parts[:half], parts[half:])]).astype(jnp.bfloat16)
            came = swap(sent, 2 * half)
            parts = [
                jnp.where(high, b, a) + came[i].astype(jnp.float32)
                for i, (a, b) in enumerate(zip(parts[:half], parts[half:]))
            ]
        return parts[0]

    arrived = []
    for kind in classes:
        held = sum_xs(pair_sums[kind]).astype(jnp.bfloat16)
        moves = [
            (d * owners + t, ring[(p - kept[kind][t]) % groups] * owners + d // per_owner)
            for p, d in enumerate(ring)
            for t in range(owners)
        ]
        arrived.append(lax.ppermute(held, ("dp", "tensor"), moves))
    own_top = pl.pallas_call(
        functools.partial(top_body, groups, classes, width),
        out_shape=jax.ShapeDtypeStruct((tokens, features), jnp.bfloat16),
        in_specs=[VMEM] * (len(classes) + 1),
        out_specs=VMEM,
        name="add_residual",
    )(*arrived, residual)

    deep_sum = jnp.dot(low_all, join_weight[0], preferred_element_type=jnp.float32)
    deep_sum = deep_sum + jnp.dot(mid_all, join_weight[1], preferred_element_type=jnp.float32)
    deep_sum = deep_sum.reshape(groups, tokens, width)
    top = Gather(own_top, 0)
    cuts = [0] + list(range(3, groups, 2)) + [groups]
    chunks = []

    def start_chunk():
        part = offsets[cuts[len(chunks)] : cuts[len(chunks) + 1]]
        total = product([top.slots[k] for k in part], join_weight[2])
        total = total + jnp.stack([pick(deep_sum, group_at[0, offsets.index(k)]) for k in part])
        chunks.append([total])

    def step_chunk(chunk):
        if len(chunk) == 1:
            by_owner = chunk[0].reshape(chunk[0].shape[0], xs, 2, rows, width)
            kept_part = lax.dynamic_index_in_dim(by_owner, core, 2, keepdims=False)
            sent_part = lax.dynamic_index_in_dim(by_owner, 1 - core, 2, keepdims=False)
            chunk.append(kept_part + swap(sent_part, 1))
        elif len(chunk) == 2:
            part, half = chunk[1], xs // 2
            while half:
                part = part.reshape((part.shape[0], 2, half) + part.shape[-2:])
                side = bit_of_x(half)
                part = lax.dynamic_index_in_dim(part, side, 1, keepdims=False) + swap(
                    lax.dynamic_index_in_dim(part, 1 - side, 1, keepdims=False), 2 * half
                )
                half //= 2
            chunk.append(part.reshape(part.shape[0], rows, width))

    while top.hops < last:
        top.hop([chunk[-1] for chunk in chunks])
        for chunk in chunks:
            step_chunk(chunk)
        while last - 2 < top.hops and len(chunks) < top.hops - 1:
            start_chunk()
            step_chunk(chunks[-1])
    while len(chunks) < len(cuts) - 1:
        start_chunk()
    for chunk in chunks:
        while len(chunk) < 3:
            step_chunk(chunk)

    owned = [part for chunk in chunks for part in chunk[-1]]
    for i, k in enumerate(offsets):
        if k:
            moves = [(ring[q], ring[(q - k) % groups]) for q in range(groups)]
            owned[i] = lax.ppermute(owned[i].astype(jnp.bfloat16), "dp", moves)
    return pl.pallas_call(
        functools.partial(norm_body, offsets, width),
        out_shape=jax.ShapeDtypeStruct((rows, groups * width), jnp.bfloat16),
        in_specs=[VMEM] * (groups + 1),
        out_specs=VMEM,
        name="norm_rows",
    )(*owned, join_gain.reshape(1, groups * width))


def solution(mesh):
    return jax.shard_map(
        local,
        mesh=mesh,
        in_specs=(
            P("dp", "tensor"),
            P("dp", "tensor"),
            P("dp", "tensor"),
            P("dp", "tensor"),
            P("tensor", "dp"),
            P(None, "tensor", "dp"),
            P(),
        ),
        out_specs=P(("dp", "tensor"), None),
        check_vma=False,
    )
```

```python
import functools

import jax
import jax.numpy as jnp
from jax import lax
from jax.experimental import pallas as pl
from jax.experimental.pallas import tpu as pltpu
from jax.sharding import PartitionSpec as P


def ring_of(groups):
    half = groups // 2
    return [2 * q for q in range(half)] + [2 * q + 1 for q in reversed(range(half))]


def tie(values, after):
    flat, tree = jax.tree.flatten(values)
    held = lax.optimization_barrier(tuple(flat) + tuple(jax.tree.leaves(after)))
    return jax.tree.unflatten(tree, held[: len(flat)])


def pick(values, index):
    return lax.dynamic_index_in_dim(values, index, 0, keepdims=False)


def place_on_ring(groups):
    dp = lax.axis_index("dp")
    return jnp.where(lax.rem(dp, 2) == 0, lax.div(dp, 2), groups - 1 - lax.div(dp, 2))


def top_body(groups, classes, width, *refs):
    arrived, rest_ref, top_ref = refs[: len(classes)], refs[-2], refs[-1]
    home = lax.axis_index("tensor") + place_on_ring(groups)
    for kind, piece_ref in zip(classes, arrived):
        j = lax.rem(home + kind, len(classes))
        columns = pl.ds(pl.multiple_of(j * width, width), width)
        total = rest_ref[:, columns].astype(jnp.float32) + piece_ref[...].astype(jnp.float32)
        top_ref[:, columns] = total.astype(jnp.bfloat16)


def norm_body(offsets, counts, width, *refs):
    groups = len(offsets)
    gain_ref, out_ref = refs[-2:]
    place = place_on_ring(groups)
    blocks, total, first = [], 0.0, 0
    for count in counts:
        block = sum(ref[...].astype(jnp.float32) for ref in refs[first : first + count])
        total = total + jnp.sum(block * block, axis=1, keepdims=True)
        blocks.append(block)
        first += count
    inverse_rms = lax.rsqrt(total / (groups * width) + 1e-05)
    for offset, block in zip(offsets, blocks):
        q = lax.rem(place + offset + groups, groups)
        d = jnp.where(q < groups // 2, 2 * q, 2 * (groups - 1 - q) + 1)
        columns = pl.ds(pl.multiple_of(d * width, width), width)
        out_ref[:, columns] = (block * inverse_rms * gain_ref[:, columns]).astype(jnp.bfloat16)


VMEM = pl.BlockSpec(memory_space=pltpu.VMEM)


class Gather:
    def __init__(self, own, axis):
        self.ring = ring_of(lax.axis_size("dp"))
        self.axis, self.last, self.hops = axis, len(self.ring) // 2, 0
        self.ends = [own, own]
        self.slots = {0: [own]}

    def hop(self):
        count = len(self.ring)
        ends = self.ends
        self.hops += 1
        if self.hops == self.last:
            middle = ends[0].shape[self.axis] // 2
            ends = [
                lax.slice_in_dim(ends[0], 0, middle, axis=self.axis),
                lax.slice_in_dim(ends[1], middle, 2 * middle, axis=self.axis),
            ]
        up = [(self.ring[q], self.ring[(q + 1) % count]) for q in range(count)]
        down = [(target, source) for source, target in up]
        self.ends = [lax.ppermute(ends[0], "dp", up), lax.ppermute(ends[1], "dp", down)]
        if self.hops == self.last:
            self.slots[self.hops] = self.ends
        else:
            self.slots[self.hops], self.slots[-self.hops] = [self.ends[0]], [self.ends[1]]


def local(attn_heads, residual, low_hidden, mid_hidden, out_weight, join_weight, join_gain):
    groups, owners = lax.axis_size("dp"), lax.axis_size("tensor")
    tokens, features = attn_heads.shape
    width = out_weight.shape[1]
    xs = owners // 2
    rows = tokens // owners
    ring = ring_of(groups)
    last = groups // 2
    offsets = [0] + [sign * s for s in range(1, last) for sign in (1, -1)] + [last]
    tensor = lax.axis_index("tensor").astype(jnp.uint32)
    core, x = tensor & 1, tensor >> 1

    def swap(values, bit):
        return lax.ppermute(values, "tensor", [(t, t ^ bit) for t in range(owners)])

    def product(slots, weight):
        rows_in = jnp.concatenate([piece for slot in slots for piece in slot], axis=0)
        return jnp.dot(rows_in, weight, preferred_element_type=jnp.float32).reshape(len(slots), tokens, width)

    def bit_of_x(half):
        return (x >> (half.bit_length() - 1)) & 1

    attn = Gather(attn_heads, 0)
    per_owner = groups // owners
    classes = list(reversed(range(per_owner)))
    kept = {kind: [k for k in offsets if k % per_owner == kind] for kind in classes}
    pair_sums = {kind: [] for kind in classes}

    def sum_pairs():
        for kind in classes:
            while len(pair_sums[kind]) < xs:
                i = 2 * len(pair_sums[kind])
                pair = kept[kind][i : i + 2]
                if not all(k in attn.slots for k in pair):
                    break
                products = product([attn.slots[k] for k in pair], out_weight)
                pair_sums[kind].append(pick(products, core) + swap(pick(products, 1 - core), 1))

    while attn.hops < last:
        ready = [list(pair_sums[kind]) for kind in classes]
        if attn.hops:
            sum_pairs()
        attn.ends = tie(attn.ends, ready)
        attn.hop()
    deep = Gather(jnp.stack([low_hidden, mid_hidden]), 1)
    deep.ends = tie(deep.ends, attn.ends)
    deep.hop()
    attn.slots[last] = tie(attn.ends, [list(pair_sums[kind]) for kind in classes])
    sum_pairs()

    def sum_xs(parts):
        while len(parts) > 1:
            half = len(parts) // 2
            high = bit_of_x(half) == 1
            sent = jnp.stack([jnp.where(high, a, b) for a, b in zip(parts[:half], parts[half:])]).astype(jnp.bfloat16)
            came = swap(sent, 2 * half)
            parts = [
                jnp.where(high, b, a) + came[i].astype(jnp.float32)
                for i, (a, b) in enumerate(zip(parts[:half], parts[half:]))
            ]
        return parts[0]

    arrived = []
    for kind in classes:
        held = sum_xs(pair_sums[kind]).astype(jnp.bfloat16)
        moves = [
            (d * owners + t, ring[(p - kept[kind][t]) % groups] * owners + d // per_owner)
            for p, d in enumerate(ring)
            for t in range(owners)
        ]
        arrived.append(lax.ppermute(held, ("dp", "tensor"), moves))
    own_top = pl.pallas_call(
        functools.partial(top_body, groups, classes, width),
        out_shape=jax.ShapeDtypeStruct((tokens, features), jnp.bfloat16),
        in_specs=[VMEM] * (len(classes) + 1),
        out_specs=VMEM,
        name="add_residual",
    )(*arrived, residual)

    top = Gather(own_top, 0)
    cuts = [0] + list(range(3, groups, 2)) + [groups]
    chunks = [offsets[low:high] for low, high in zip(cuts, cuts[1:])]
    deep_sums, totals, sums, owned = [], [], [], {}

    def add_deep():
        part = chunks[len(deep_sums)]
        total = product([[piece[0] for piece in deep.slots[k]] for k in part], join_weight[0])
        deep_sums.append(total + product([[piece[1] for piece in deep.slots[k]] for k in part], join_weight[1]))

    def add_top():
        n = len(totals)
        total = product([top.slots[k] for k in chunks[n]], join_weight[2]) + deep_sums[n]
        by_owner = total.reshape(len(chunks[n]), xs, 2, rows, width)
        kept_part = lax.dynamic_index_in_dim(by_owner, core, 2, keepdims=False)
        sent_part = lax.dynamic_index_in_dim(by_owner, 1 - core, 2, keepdims=False)
        totals.append(kept_part + swap(sent_part, 1))

    def send(part, k, flip=0):
        if not k and not flip:
            return part
        moves = [
            (ring[q] * owners + t, ring[(q - k) % groups] * owners + (t ^ (2 * flip)))
            for q in range(groups)
            for t in range(owners)
        ]
        return lax.ppermute(part.astype(jnp.bfloat16), ("dp", "tensor"), moves)

    def add_x():
        n = len(sums)
        part, half = totals[n], xs // 2
        while half:
            part = part.reshape((part.shape[0], 2, half) + part.shape[-2:])
            side = bit_of_x(half)
            part = lax.dynamic_index_in_dim(part, side, 1, keepdims=False) + swap(
                lax.dynamic_index_in_dim(part, 1 - side, 1, keepdims=False), 2 * half
            )
            half //= 2
        part = part.reshape(part.shape[0], rows, width)
        sums.append(part)
        for i, k in enumerate(chunks[n]):
            owned[k] = [send(part[i], k)]

    while top.hops < last:
        top.ends, deep.ends = tie((top.ends, deep.ends), [deep_sums, totals, sums])
        top.hop()
        if deep.hops < last:
            deep.hop()
        if top.hops > 1:
            add_top()
            if top.hops < last:
                add_x()
        add_deep()
    top.slots[last] = tie(top.ends, [deep_sums, totals])
    add_top()
    add_x()
    for flip in range(xs):
        part = pick(totals[-1][0], x ^ flip)
        owned.setdefault(last, []).append(send(part, last, flip))
    parts = [part for k in offsets for part in owned[k]]
    counts = [len(owned[k]) for k in offsets]
    return pl.pallas_call(
        functools.partial(norm_body, offsets, counts, width),
        out_shape=jax.ShapeDtypeStruct((rows, groups * width), jnp.bfloat16),
        in_specs=[VMEM] * (len(parts) + 1),
        out_specs=VMEM,
        name="norm_rows",
    )(*parts, join_gain.reshape(1, groups * width))


def solution(mesh):
    return jax.shard_map(
        local,
        mesh=mesh,
        in_specs=(
            P("dp", "tensor"),
            P("dp", "tensor"),
            P("dp", "tensor"),
            P("dp", "tensor"),
            P("tensor", "dp"),
            P(None, "tensor", "dp"),
            P(),
        ),
        out_specs=P(("dp", "tensor"), None),
        check_vma=False,
    )
```

```python
import functools

import jax
import jax.numpy as jnp
from jax import lax
from jax.experimental import pallas as pl
from jax.experimental.pallas import tpu as pltpu
from jax.sharding import PartitionSpec as P


def ring_of(groups):
    half = groups // 2
    return [2 * q for q in range(half)] + [2 * q + 1 for q in reversed(range(half))]


def tie(values, after):
    flat, tree = jax.tree.flatten(values)
    held = lax.optimization_barrier(tuple(flat) + tuple(jax.tree.leaves(after)))
    return jax.tree.unflatten(tree, held[: len(flat)])


def pick(values, index):
    return lax.dynamic_index_in_dim(values, index, 0, keepdims=False)


def place_on_ring(groups):
    dp = lax.axis_index("dp")
    return jnp.where(lax.rem(dp, 2) == 0, lax.div(dp, 2), groups - 1 - lax.div(dp, 2))


def top_body(groups, classes, width, *refs):
    arrived, rest_ref, top_ref = refs[: len(classes)], refs[-2], refs[-1]
    home = lax.axis_index("tensor") + place_on_ring(groups)
    for kind, piece_ref in zip(classes, arrived):
        j = lax.rem(home + kind, len(classes))
        columns = pl.ds(pl.multiple_of(j * width, width), width)
        total = rest_ref[:, columns].astype(jnp.float32) + piece_ref[...].astype(jnp.float32)
        top_ref[:, columns] = total.astype(jnp.bfloat16)


def norm_body(offsets, counts, width, *refs):
    groups = len(offsets)
    gain_ref, out_ref = refs[-2:]
    place = place_on_ring(groups)
    blocks, total, first = [], 0.0, 0
    for count in counts:
        block = sum(ref[...].astype(jnp.float32) for ref in refs[first : first + count])
        total = total + jnp.sum(block * block, axis=1, keepdims=True)
        blocks.append(block)
        first += count
    inverse_rms = lax.rsqrt(total / (groups * width) + 1e-05)
    for offset, block in zip(offsets, blocks):
        q = lax.rem(place + offset + groups, groups)
        d = jnp.where(q < groups // 2, 2 * q, 2 * (groups - 1 - q) + 1)
        columns = pl.ds(pl.multiple_of(d * width, width), width)
        out_ref[:, columns] = (block * inverse_rms * gain_ref[:, columns]).astype(jnp.bfloat16)


VMEM = pl.BlockSpec(memory_space=pltpu.VMEM)


class Gather:
    def __init__(self, own, axis):
        self.ring = ring_of(lax.axis_size("dp"))
        self.axis, self.last, self.hops = axis, len(self.ring) // 2, 0
        self.ends = [own, own]
        self.slots = {0: [own]}

    def hop(self):
        count = len(self.ring)
        ends = self.ends
        self.hops += 1
        if self.hops == self.last:
            middle = ends[0].shape[self.axis] // 2
            ends = [
                lax.slice_in_dim(ends[0], 0, middle, axis=self.axis),
                lax.slice_in_dim(ends[1], middle, 2 * middle, axis=self.axis),
            ]
        up = [(self.ring[q], self.ring[(q + 1) % count]) for q in range(count)]
        down = [(target, source) for source, target in up]
        self.ends = [lax.ppermute(ends[0], "dp", up), lax.ppermute(ends[1], "dp", down)]
        if self.hops == self.last:
            self.slots[self.hops] = self.ends
        else:
            self.slots[self.hops], self.slots[-self.hops] = [self.ends[0]], [self.ends[1]]


def local(attn_heads, residual, low_hidden, mid_hidden, out_weight, join_weight, join_gain):
    groups, owners = lax.axis_size("dp"), lax.axis_size("tensor")
    tokens, features = attn_heads.shape
    width = out_weight.shape[1]
    xs = owners // 2
    rows = tokens // owners
    ring = ring_of(groups)
    last = groups // 2
    offsets = [0] + [sign * s for s in range(1, last) for sign in (1, -1)] + [last]
    tensor = lax.axis_index("tensor").astype(jnp.uint32)
    core, x = tensor & 1, tensor >> 1

    def swap(values, bit):
        return lax.ppermute(values, "tensor", [(t, t ^ bit) for t in range(owners)])

    def product(slots, weight):
        rows_in = jnp.concatenate([piece for slot in slots for piece in slot], axis=0)
        return jnp.dot(rows_in, weight, preferred_element_type=jnp.float32).reshape(len(slots), tokens, width)

    def bit_of_x(half):
        return (x >> (half.bit_length() - 1)) & 1

    attn = Gather(attn_heads, 0)
    per_owner = groups // owners
    classes = list(reversed(range(per_owner)))
    kept = {kind: [k for k in offsets if k % per_owner == kind] for kind in classes}
    pair_sums = {kind: [] for kind in classes}

    done_pairs = {kind: 0 for kind in classes}

    def multiply_pairs(reach):
        made = {kind: [] for kind in classes}
        for kind in classes:
            while done_pairs[kind] < xs:
                i = 2 * done_pairs[kind]
                pair = kept[kind][i : i + 2]
                if any(abs(k) > reach for k in pair):
                    break
                made[kind].append(product([attn.slots[k] for k in pair], out_weight))
                done_pairs[kind] += 1
        return made

    def sum_cores(products):
        return pick(products, core) + swap(pick(products, 1 - core), 1)

    low = Gather(low_hidden, 0)
    waiting = {kind: [] for kind in classes}
    for hop in range(1, last + 1):
        attn.ends, low.ends, waiting = tie((attn.ends, low.ends, waiting), ())
        attn.hop()
        low.hop()
        for kind in classes:
            pair_sums[kind] += [sum_cores(products) for products in waiting[kind]]
        waiting = multiply_pairs(hop - 1)
    mid = Gather(mid_hidden, 0)
    mid.ends = tie(mid.ends, attn.ends)
    mid.hop()
    for part in (waiting, multiply_pairs(last)):
        for kind in classes:
            pair_sums[kind] += [sum_cores(products) for products in part[kind]]

    def sum_xs(parts):
        while len(parts) > 1:
            half = len(parts) // 2
            high = bit_of_x(half) == 1
            sent = jnp.stack([jnp.where(high, a, b) for a, b in zip(parts[:half], parts[half:])]).astype(jnp.bfloat16)
            came = swap(sent, 2 * half)
            parts = [
                jnp.where(high, b, a) + came[i].astype(jnp.float32)
                for i, (a, b) in enumerate(zip(parts[:half], parts[half:]))
            ]
        return parts[0]

    arrived = []
    for kind in classes:
        held = sum_xs(pair_sums[kind]).astype(jnp.bfloat16)
        moves = [
            (d * owners + t, ring[(p - kept[kind][t]) % groups] * owners + d // per_owner)
            for p, d in enumerate(ring)
            for t in range(owners)
        ]
        arrived.append(lax.ppermute(held, ("dp", "tensor"), moves))
    own_top = pl.pallas_call(
        functools.partial(top_body, groups, classes, width),
        out_shape=jax.ShapeDtypeStruct((tokens, features), jnp.bfloat16),
        in_specs=[VMEM] * (len(classes) + 1),
        out_specs=VMEM,
        name="add_residual",
    )(*arrived, residual)

    top = Gather(own_top, 0)
    cuts = [0] + list(range(3, groups, 2)) + [groups]
    chunks = [offsets[low_cut:high_cut] for low_cut, high_cut in zip(cuts, cuts[1:])]
    owned = {}

    def multiply(part):
        total = product([low.slots[k] for k in part], join_weight[0])
        total = total + product([mid.slots[k] for k in part], join_weight[1])
        return total + product([top.slots[k] for k in part], join_weight[2])

    def add_cores(total):
        by_owner = total.reshape(total.shape[0], xs, 2, rows, width)
        kept_part = lax.dynamic_index_in_dim(by_owner, core, 2, keepdims=False)
        sent_part = lax.dynamic_index_in_dim(by_owner, 1 - core, 2, keepdims=False)
        return kept_part + swap(sent_part, 1)

    def send(part, k, flip=0):
        if not k and not flip:
            return part
        moves = [
            (ring[q] * owners + t, ring[(q - k) % groups] * owners + (t ^ (2 * flip)))
            for q in range(groups)
            for t in range(owners)
        ]
        return lax.ppermute(part.astype(jnp.bfloat16), ("dp", "tensor"), moves)

    def add_x(part, total):
        half = xs // 2
        while half:
            total = total.reshape((total.shape[0], 2, half) + total.shape[-2:])
            side = bit_of_x(half)
            total = lax.dynamic_index_in_dim(total, side, 1, keepdims=False) + swap(
                lax.dynamic_index_in_dim(total, 1 - side, 1, keepdims=False), 2 * half
            )
            half //= 2
        total = total.reshape(total.shape[0], rows, width)
        for i, k in enumerate(part):
            owned[k] = [send(total[i], k)]

    def add_halves(part, total):
        for flip in range(xs):
            for i, k in enumerate(part):
                owned.setdefault(k, []).append(send(pick(total[i], x ^ flip), k, flip))

    cored = {}
    for hop in range(1, last + 1):
        top.ends, mid.ends, cored = tie((top.ends, mid.ends, cored), low.ends)
        top.hop()
        if mid.hops < last:
            mid.hop()
        for n, total in cored.items():
            add_x(chunks[n], total)
        cored = {hop - 2: add_cores(multiply(chunks[hop - 2]))} if hop > 1 else {}
    for n, total in cored.items():
        add_halves(chunks[n], total)
    add_halves(chunks[-1], add_cores(multiply(chunks[-1])))
    parts = [part for k in offsets for part in owned[k]]
    counts = [len(owned[k]) for k in offsets]
    return pl.pallas_call(
        functools.partial(norm_body, offsets, counts, width),
        out_shape=jax.ShapeDtypeStruct((rows, groups * width), jnp.bfloat16),
        in_specs=[VMEM] * (len(parts) + 1),
        out_specs=VMEM,
        name="norm_rows",
    )(*parts, join_gain.reshape(1, groups * width))


def solution(mesh):
    return jax.shard_map(
        local,
        mesh=mesh,
        in_specs=(
            P("dp", "tensor"),
            P("dp", "tensor"),
            P("dp", "tensor"),
            P("dp", "tensor"),
            P("tensor", "dp"),
            P(None, "tensor", "dp"),
            P(),
        ),
        out_specs=P(("dp", "tensor"), None),
        check_vma=False,
    )
```

```python
import functools

import jax
import jax.numpy as jnp
from jax import lax
from jax.experimental import pallas as pl
from jax.experimental.pallas import tpu as pltpu
from jax.sharding import PartitionSpec as P


def ring_of(groups):
    half = groups // 2
    return [2 * q for q in range(half)] + [2 * q + 1 for q in reversed(range(half))]


def tie(*values):
    flat, tree = jax.tree.flatten(values)
    return jax.tree.unflatten(tree, lax.optimization_barrier(tuple(flat)))


def pick(values, index):
    return lax.dynamic_index_in_dim(values, index, 0, keepdims=False)


def place_on_ring(groups):
    dp = lax.axis_index("dp")
    return jnp.where(lax.rem(dp, 2) == 0, lax.div(dp, 2), groups - 1 - lax.div(dp, 2))


def top_body(groups, classes, width, *refs):
    arrived, rest_ref, top_ref = refs[: len(classes)], refs[-2], refs[-1]
    home = lax.axis_index("tensor") + place_on_ring(groups)
    for kind, piece_ref in zip(classes, arrived):
        j = lax.rem(home + kind, len(classes))
        columns = pl.ds(pl.multiple_of(j * width, width), width)
        total = rest_ref[:, columns].astype(jnp.float32) + piece_ref[...].astype(jnp.float32)
        top_ref[:, columns] = total.astype(jnp.bfloat16)


def norm_body(offsets, counts, width, *refs):
    groups = len(offsets)
    gain_ref, out_ref = refs[-2:]
    place = place_on_ring(groups)
    blocks, total, first = [], 0.0, 0
    for count in counts:
        block = sum(ref[...].astype(jnp.float32) for ref in refs[first : first + count])
        total = total + jnp.sum(block * block, axis=1, keepdims=True)
        blocks.append(block)
        first += count
    inverse_rms = lax.rsqrt(total / (groups * width) + 1e-05)
    for offset, block in zip(offsets, blocks):
        q = lax.rem(place + offset + groups, groups)
        d = jnp.where(q < groups // 2, 2 * q, 2 * (groups - 1 - q) + 1)
        columns = pl.ds(pl.multiple_of(d * width, width), width)
        out_ref[:, columns] = (block * inverse_rms * gain_ref[:, columns]).astype(jnp.bfloat16)


VMEM = pl.BlockSpec(memory_space=pltpu.VMEM)


class Gather:
    def __init__(self, own, axis):
        self.ring = ring_of(lax.axis_size("dp"))
        self.axis, self.last, self.hops = axis, len(self.ring) // 2, 0
        self.ends = [own, own]
        self.slots = {0: [own]}

    def hop(self):
        count = len(self.ring)
        ends = self.ends
        self.hops += 1
        if self.hops == self.last:
            middle = ends[0].shape[self.axis] // 2
            ends = [
                lax.slice_in_dim(ends[0], 0, middle, axis=self.axis),
                lax.slice_in_dim(ends[1], middle, 2 * middle, axis=self.axis),
            ]
        up = [(self.ring[q], self.ring[(q + 1) % count]) for q in range(count)]
        down = [(target, source) for source, target in up]
        self.ends = [lax.ppermute(ends[0], "dp", up), lax.ppermute(ends[1], "dp", down)]
        if self.hops == self.last:
            self.slots[self.hops] = self.ends
        else:
            self.slots[self.hops], self.slots[-self.hops] = [self.ends[0]], [self.ends[1]]


def local(attn_heads, residual, low_hidden, mid_hidden, out_weight, join_weight, join_gain):
    groups, owners = lax.axis_size("dp"), lax.axis_size("tensor")
    tokens, features = attn_heads.shape
    width = out_weight.shape[1]
    xs = owners // 2
    rows = tokens // owners
    ring = ring_of(groups)
    last = groups // 2
    offsets = [0] + [sign * s for s in range(1, last) for sign in (1, -1)] + [last]
    tensor = lax.axis_index("tensor").astype(jnp.uint32)
    core, x = tensor & 1, tensor >> 1

    def swap(values, bit):
        return lax.ppermute(values, "tensor", [(t, t ^ bit) for t in range(owners)])

    def product(slots, weight):
        rows_in = jnp.concatenate([piece for slot in slots for piece in slot], axis=0)
        return jnp.dot(rows_in, weight, preferred_element_type=jnp.float32).reshape(len(slots), tokens, width)

    def bit_of_x(half):
        return (x >> (half.bit_length() - 1)) & 1

    attn = Gather(attn_heads, 0)
    per_owner = groups // owners
    classes = list(reversed(range(per_owner)))
    kept = {kind: [k for k in offsets if k % per_owner == kind] for kind in classes}
    kept = {kind: slots[-1:] + slots[:-1] for kind, slots in kept.items()}
    pair_sums = {kind: [None] * xs for kind in classes}

    def multiply_pairs(reach):
        made = {}
        for kind in classes:
            for i in range(xs):
                pair = kept[kind][2 * i : 2 * i + 2]
                if max(abs(k) for k in pair) == reach:
                    made[kind, i] = product([attn.slots[k] for k in pair], out_weight)
        return made

    def sum_cores(made):
        for (kind, i), products in made.items():
            pair_sums[kind][i] = pick(products, core) + swap(pick(products, 1 - core), 1)

    low = Gather(low_hidden, 0)
    mid = Gather(mid_hidden, 0)
    made = {}
    for hop in range(1, last + 1):
        attn.ends, low.ends, mid.ends, values = tie(attn.ends, low.ends, mid.ends, list(made.values()))
        made = dict(zip(made, values))
        attn.hop()
        (mid if hop == last else low).hop()
        sum_cores(made)
        made = multiply_pairs(hop - 1)
    low.ends, attn.ends = tie(low.ends, attn.ends)
    low.hop()
    sum_cores(made)
    attn.slots[last], pair_sums = tie(attn.ends, pair_sums)
    sum_cores(multiply_pairs(last))

    def sum_xs(parts):
        while len(parts) > 1:
            half = len(parts) // 2
            high = bit_of_x(half) == 1
            sent = jnp.stack([jnp.where(high, a, b) for a, b in zip(parts[:half], parts[half:])]).astype(jnp.bfloat16)
            came = swap(sent, 2 * half)
            parts = [
                jnp.where(high, b, a) + came[i].astype(jnp.float32)
                for i, (a, b) in enumerate(zip(parts[:half], parts[half:]))
            ]
        return parts[0]

    arrived = []
    for kind in classes:
        held, mid.ends = tie(sum_xs(pair_sums[kind]).astype(jnp.bfloat16), mid.ends)
        moves = [
            (d * owners + t, ring[(p - kept[kind][t]) % groups] * owners + d // per_owner)
            for p, d in enumerate(ring)
            for t in range(owners)
        ]
        arrived.append(lax.ppermute(held, ("dp", "tensor"), moves))
    own_top = pl.pallas_call(
        functools.partial(top_body, groups, classes, width),
        out_shape=jax.ShapeDtypeStruct((tokens, features), jnp.bfloat16),
        in_specs=[VMEM] * (len(classes) + 1),
        out_specs=VMEM,
        name="add_residual",
    )(*arrived, residual)

    own_top, low.slots[last] = tie(own_top, low.slots[last])
    top = Gather(own_top, 0)
    cuts = [0] + list(range(3, groups, 2)) + [groups]
    chunks = [offsets[low_cut:high_cut] for low_cut, high_cut in zip(cuts, cuts[1:])]
    owned = {}

    def multiply_deep(part):
        total = product([low.slots[k] for k in part], join_weight[0])
        return total + product([mid.slots[k] for k in part], join_weight[1])

    def multiply(part, deep_sum):
        return product([top.slots[k] for k in part], join_weight[2]) + deep_sum

    def add_cores(total):
        by_owner = total.reshape(total.shape[0], xs, 2, rows, width)
        kept_part = lax.dynamic_index_in_dim(by_owner, core, 2, keepdims=False)
        sent_part = lax.dynamic_index_in_dim(by_owner, 1 - core, 2, keepdims=False)
        return kept_part + swap(sent_part, 1)

    def send(part, k, flip=0):
        if not k and not flip:
            return part
        moves = [
            (ring[q] * owners + t, ring[(q - k) % groups] * owners + (t ^ (2 * flip)))
            for q in range(groups)
            for t in range(owners)
        ]
        return lax.ppermute(part.astype(jnp.bfloat16), ("dp", "tensor"), moves)

    def add_x(part, total, dtype):
        half = xs // 2
        while half:
            total = total.reshape((total.shape[0], 2, half) + total.shape[-2:])
            side = bit_of_x(half)
            sent = lax.dynamic_index_in_dim(total, 1 - side, 1, keepdims=False).astype(dtype)
            total = lax.dynamic_index_in_dim(total, side, 1, keepdims=False) + swap(sent, 2 * half).astype(jnp.float32)
            half //= 2
        total = total.reshape(total.shape[0], rows, width)
        for i, k in enumerate(part):
            owned[k] = [send(total[i], k)]

    def add_halves(part, total):
        for flip in range(xs):
            for i, k in enumerate(part):
                owned.setdefault(k, []).append(send(pick(total[i], x ^ flip), k, flip))

    cored, deep_sum = {}, None
    for hop in range(1, last + 1):
        top.ends, mid.ends, cored, deep_sum = tie(top.ends, mid.ends, cored, deep_sum)
        top.hop()
        if mid.hops < last:
            mid.hop()
        for n, total in cored.items():
            add_x(chunks[n], total, jnp.float32 if n == 0 else jnp.bfloat16)
        cored = {hop - 2: add_cores(multiply(chunks[hop - 2], deep_sum))} if hop > 1 else {}
        deep_sum = multiply_deep(chunks[hop - 1])
    for n, total in cored.items():
        add_x(chunks[n], total, jnp.bfloat16)
    early = {k: owned[k] for part in chunks[:-2] for k in part}
    top.slots[last], early, deep_sum = tie(top.ends, early, deep_sum)
    owned.update(early)
    add_halves(chunks[-1], add_cores(multiply(chunks[-1], deep_sum)))
    parts = [part for k in offsets for part in owned[k]]
    counts = [len(owned[k]) for k in offsets]
    return pl.pallas_call(
        functools.partial(norm_body, offsets, counts, width),
        out_shape=jax.ShapeDtypeStruct((rows, groups * width), jnp.bfloat16),
        in_specs=[VMEM] * (len(parts) + 1),
        out_specs=VMEM,
        name="norm_rows",
    )(*parts, join_gain.reshape(1, groups * width))


def solution(mesh):
    return jax.shard_map(
        local,
        mesh=mesh,
        in_specs=(
            P("dp", "tensor"),
            P("dp", "tensor"),
            P("dp", "tensor"),
            P("dp", "tensor"),
            P("tensor", "dp"),
            P(None, "tensor", "dp"),
            P(),
        ),
        out_specs=P(("dp", "tensor"), None),
        check_vma=False,
    )
```

```python
import functools

import jax
import jax.numpy as jnp
from jax import lax
from jax.experimental import pallas as pl
from jax.experimental.pallas import tpu as pltpu
from jax.sharding import PartitionSpec as P


def ring_of(groups):
    half = groups // 2
    return [2 * q for q in range(half)] + [2 * q + 1 for q in reversed(range(half))]


def tie(*values):
    flat, tree = jax.tree.flatten(values)
    return jax.tree.unflatten(tree, lax.optimization_barrier(tuple(flat)))


def pick(values, index):
    return lax.dynamic_index_in_dim(values, index, 0, keepdims=False)


def place_on_ring(groups):
    dp = lax.axis_index("dp")
    return jnp.where(lax.rem(dp, 2) == 0, lax.div(dp, 2), groups - 1 - lax.div(dp, 2))


def top_body(groups, classes, width, *refs):
    arrived, rest_ref, top_ref = refs[: len(classes)], refs[-2], refs[-1]
    home = lax.axis_index("tensor") + place_on_ring(groups)
    for kind, piece_ref in zip(classes, arrived):
        j = lax.rem(home + kind, len(classes))
        columns = pl.ds(pl.multiple_of(j * width, width), width)
        total = rest_ref[:, columns].astype(jnp.float32) + piece_ref[...].astype(jnp.float32)
        top_ref[:, columns] = total.astype(jnp.bfloat16)


def norm_body(offsets, counts, width, *refs):
    groups = len(offsets)
    gain_ref, out_ref = refs[-2:]
    place = place_on_ring(groups)
    blocks, total, first = [], 0.0, 0
    for count in counts:
        block = sum(ref[...].astype(jnp.float32) for ref in refs[first : first + count])
        total = total + jnp.sum(block * block, axis=1, keepdims=True)
        blocks.append(block)
        first += count
    inverse_rms = lax.rsqrt(total / (groups * width) + 1e-05)
    for offset, block in zip(offsets, blocks):
        q = lax.rem(place + offset + groups, groups)
        d = jnp.where(q < groups // 2, 2 * q, 2 * (groups - 1 - q) + 1)
        columns = pl.ds(pl.multiple_of(d * width, width), width)
        out_ref[:, columns] = (block * inverse_rms * gain_ref[:, columns]).astype(jnp.bfloat16)


VMEM = pl.BlockSpec(memory_space=pltpu.VMEM)


class Gather:
    def __init__(self, own):
        self.ring = ring_of(lax.axis_size("dp"))
        self.last, self.hops = len(self.ring) // 2, 0
        self.ends = [own, own]
        self.slots = {0: [own]}

    def halves(self):
        middle = self.ends[0].shape[0] // 2
        return [self.ends[0][:middle], self.ends[1][middle:]]

    def hop(self):
        count = len(self.ring)
        ends = self.ends
        self.hops += 1
        if self.hops == self.last:
            ends = self.halves()
        up = [(self.ring[q], self.ring[(q + 1) % count]) for q in range(count)]
        down = [(target, source) for source, target in up]
        self.ends = [lax.ppermute(ends[0], "dp", up), lax.ppermute(ends[1], "dp", down)]
        if self.hops == self.last:
            self.slots[self.hops] = self.ends
        else:
            self.slots[self.hops], self.slots[-self.hops] = [self.ends[0]], [self.ends[1]]


def local(attn_heads, residual, low_hidden, mid_hidden, out_weight, join_weight, join_gain):
    groups, owners = lax.axis_size("dp"), lax.axis_size("tensor")
    tokens, features = attn_heads.shape
    width = out_weight.shape[1]
    xs = owners // 2
    rows = tokens // owners
    ring = ring_of(groups)
    last = groups // 2
    offsets = [0] + [sign * s for s in range(1, last) for sign in (1, -1)] + [last]
    tensor = lax.axis_index("tensor").astype(jnp.uint32)
    core, x = tensor & 1, tensor >> 1

    def swap(values, bit):
        return lax.ppermute(values, "tensor", [(t, t ^ bit) for t in range(owners)])

    def product(slots, weight):
        rows_in = jnp.concatenate([piece for slot in slots for piece in slot], axis=0)
        return jnp.dot(rows_in, weight, preferred_element_type=jnp.float32).reshape(len(slots), tokens, width)

    def bit_of_x(half):
        return (x >> (half.bit_length() - 1)) & 1

    attn = Gather(attn_heads)
    per_owner = groups // owners
    classes = list(reversed(range(per_owner)))
    kept = {kind: [k for k in offsets if k % per_owner == kind] for kind in classes}
    kept = {kind: slots[-1:] + slots[:-1] for kind, slots in kept.items()}
    pair_sums = {kind: [None] * xs for kind in classes}

    parts = {}

    def multiply_slots(slots):
        products = product([attn.slots[k] for k in slots], out_weight)
        parts.update({k: products[n] for n, k in enumerate(slots)})

    def sum_cores(reach):
        ready = []
        for kind in classes:
            for i, pair in enumerate(zip(kept[kind][::2], kept[kind][1::2])):
                if pair_sums[kind][i] is None and max(abs(k) for k in pair) <= reach:
                    ready.append((kind, i, parts[pair[0]], parts[pair[1]]))
        came = swap(jnp.stack([jnp.where(core == 0, second, first) for _, _, first, second in ready]), 1)
        for n, (kind, i, first, second) in enumerate(ready):
            pair_sums[kind][i] = jnp.where(core == 0, first, second) + came[n]

    low = Gather(low_hidden)
    mid = Gather(mid_hidden)
    for hop in range(1, last + 1):
        attn.ends, low.ends, mid.ends, parts = tie(attn.ends, low.ends, mid.ends, parts)
        attn.hop()
        (mid if hop == last else low).hop()
        if hop == 2:
            multiply_slots([0])
        if hop > 1:
            multiply_slots([hop - 1, 1 - hop])
    sum_cores(last - 1)
    attn.slots[last], pair_sums = tie(attn.ends, pair_sums)
    multiply_slots([last])
    sum_cores(last)

    def sum_xs(parts):
        while len(parts) > 1:
            half = len(parts) // 2
            high = bit_of_x(half) == 1
            sent = jnp.stack([jnp.where(high, a, b) for a, b in zip(parts[:half], parts[half:])]).astype(jnp.bfloat16)
            came = swap(sent, 2 * half)
            parts = [
                jnp.where(high, b, a) + came[i].astype(jnp.float32)
                for i, (a, b) in enumerate(zip(parts[:half], parts[half:]))
            ]
        return parts[0]

    arrived = []
    for kind in classes:
        held = sum_xs(pair_sums[kind]).astype(jnp.bfloat16)
        if kind == classes[-1]:
            held, mid.ends = tie(held, mid.ends)
        moves = [
            (d * owners + t, ring[(p - kept[kind][t]) % groups] * owners + d // per_owner)
            for p, d in enumerate(ring)
            for t in range(owners)
        ]
        arrived.append(lax.ppermute(held, ("dp", "tensor"), moves))
    own_top = pl.pallas_call(
        functools.partial(top_body, groups, classes, width),
        out_shape=jax.ShapeDtypeStruct((tokens, features), jnp.bfloat16),
        in_specs=[VMEM] * (len(classes) + 1),
        out_specs=VMEM,
        name="add_residual",
    )(*arrived, residual)

    own_top, mid.ends, mid.slots = tie(own_top, mid.ends, mid.slots)
    top = Gather(own_top)
    cuts = [0] + list(range(3, groups, 2)) + [groups]
    chunks = [offsets[low_cut:high_cut] for low_cut, high_cut in zip(cuts, cuts[1:])]
    owned = {}

    def multiply(part, depth, weight):
        return product([depth.slots[k] for k in part], weight)

    def add_cores(total):
        by_owner = total.reshape(total.shape[0], xs, 2, rows, width)
        kept_part = lax.dynamic_index_in_dim(by_owner, core, 2, keepdims=False)
        sent_part = lax.dynamic_index_in_dim(by_owner, 1 - core, 2, keepdims=False)
        return kept_part + swap(sent_part, 1)

    def send(part, k, flip=0):
        if not k and not flip:
            return part
        moves = [
            (ring[q] * owners + t, ring[(q - k) % groups] * owners + (t ^ (2 * flip)))
            for q in range(groups)
            for t in range(owners)
        ]
        return lax.ppermute(part.astype(jnp.bfloat16), ("dp", "tensor"), moves)

    def add_x(total):
        half = xs // 2
        while half:
            total = total.reshape((total.shape[0], 2, half) + total.shape[-2:])
            side = bit_of_x(half)
            sent = lax.dynamic_index_in_dim(total, 1 - side, 1, keepdims=False).astype(jnp.bfloat16)
            total = lax.dynamic_index_in_dim(total, side, 1, keepdims=False) + swap(sent, 2 * half).astype(jnp.float32)
            half //= 2
        return total.reshape(total.shape[0], rows, width)

    def send_all(part, total):
        for i, k in enumerate(part):
            owned[k] = [send(total[i], k)]

    def add_halves(part, total):
        for flip in range(xs):
            for i, k in enumerate(part):
                owned.setdefault(k, []).append(send(pick(total[i], x ^ flip), k, flip))

    def last_hops(*gathers):
        joint = Gather(None)
        joint.hops = last - 1
        joint.halves = lambda: [jnp.concatenate(ends) for ends in zip(*[gather.halves() for gather in gathers])]
        joint.hop()
        for gather, *pieces in zip(gathers, *[jnp.split(end, len(gathers)) for end in joint.ends]):
            gather.slots[last] = pieces

    deep_sum, cored = None, None
    for hop in range(1, last + 1):
        top.ends, mid.ends, low.ends, deep_sum, cored, owned = tie(
            top.ends, mid.ends, low.ends, deep_sum, cored, owned
        )
        top.hop()
        if hop < last - 1:
            mid.hop()
        elif hop == last:
            last_hops(low, mid)
        if hop > 2:
            send_all(chunks[hop - 3], add_x(cored))
        if hop > 1:
            cored = add_cores(multiply(chunks[hop - 2], top, join_weight[2]) + deep_sum)
        if hop < last:
            deep_sum = multiply(chunks[hop - 1], low, join_weight[0]) + multiply(chunks[hop - 1], mid, join_weight[1])
    add_halves(chunks[-2], cored)
    deep_sum = multiply(chunks[-1], low, join_weight[0]) + multiply(chunks[-1], mid, join_weight[1])
    add_halves(chunks[-1], add_cores(multiply(chunks[-1], top, join_weight[2]) + deep_sum))
    blocks = [part for k in offsets for part in owned[k]]
    counts = [len(owned[k]) for k in offsets]
    return pl.pallas_call(
        functools.partial(norm_body, offsets, counts, width),
        out_shape=jax.ShapeDtypeStruct((rows, groups * width), jnp.bfloat16),
        in_specs=[VMEM] * (len(blocks) + 1),
        out_specs=VMEM,
        name="norm_rows",
    )(*blocks, join_gain.reshape(1, groups * width))


def solution(mesh):
    return jax.shard_map(
        local,
        mesh=mesh,
        in_specs=(
            P("dp", "tensor"),
            P("dp", "tensor"),
            P("dp", "tensor"),
            P("dp", "tensor"),
            P("tensor", "dp"),
            P(None, "tensor", "dp"),
            P(),
        ),
        out_specs=P(("dp", "tensor"), None),
        check_vma=False,
    )
```

```python
import functools

import jax
import jax.numpy as jnp
from jax import lax
from jax.experimental import pallas as pl
from jax.experimental.pallas import tpu as pltpu
from jax.sharding import PartitionSpec as P


def ring_of(groups):
    half = groups // 2
    return [2 * q for q in range(half)] + [2 * q + 1 for q in reversed(range(half))]


def tie(*values):
    flat, tree = jax.tree.flatten(values)
    return jax.tree.unflatten(tree, lax.optimization_barrier(tuple(flat)))


def pick(values, index):
    return lax.dynamic_index_in_dim(values, index, 0, keepdims=False)


def place_on_ring(groups):
    dp = lax.axis_index("dp")
    return jnp.where(lax.rem(dp, 2) == 0, lax.div(dp, 2), groups - 1 - lax.div(dp, 2))


def top_body(groups, classes, width, *refs):
    arrived, rest_ref, top_ref = refs[: len(classes)], refs[-2], refs[-1]
    home = lax.axis_index("tensor") + place_on_ring(groups)
    for kind, piece_ref in zip(classes, arrived):
        j = lax.rem(home + kind, len(classes))
        columns = pl.ds(pl.multiple_of(j * width, width), width)
        total = rest_ref[:, columns].astype(jnp.float32) + piece_ref[...].astype(jnp.float32)
        top_ref[:, columns] = total.astype(jnp.bfloat16)


def norm_body(offsets, counts, width, *refs):
    groups = len(offsets)
    gain_ref, out_ref = refs[-2:]
    place = place_on_ring(groups)
    blocks, total, first = [], 0.0, 0
    for count in counts:
        block = sum(ref[...].astype(jnp.float32) for ref in refs[first : first + count])
        total = total + jnp.sum(block * block, axis=1, keepdims=True)
        blocks.append(block)
        first += count
    inverse_rms = lax.rsqrt(total / (groups * width) + 1e-05)
    for offset, block in zip(offsets, blocks):
        q = lax.rem(place + offset + groups, groups)
        d = jnp.where(q < groups // 2, 2 * q, 2 * (groups - 1 - q) + 1)
        columns = pl.ds(pl.multiple_of(d * width, width), width)
        out_ref[:, columns] = (block * inverse_rms * gain_ref[:, columns]).astype(jnp.bfloat16)


VMEM = pl.BlockSpec(memory_space=pltpu.VMEM)


class Gather:
    def __init__(self, own):
        self.ring = ring_of(lax.axis_size("dp"))
        self.last, self.hops = len(self.ring) // 2, 0
        self.ends = [own, own]
        self.slots = {0: [own]}

    def halves(self):
        middle = self.ends[0].shape[0] // 2
        return [self.ends[0][:middle], self.ends[1][middle:]]

    def hop(self):
        count = len(self.ring)
        ends = self.ends
        self.hops += 1
        if self.hops == self.last:
            ends = self.halves()
        up = [(self.ring[q], self.ring[(q + 1) % count]) for q in range(count)]
        down = [(target, source) for source, target in up]
        self.ends = [lax.ppermute(ends[0], "dp", up), lax.ppermute(ends[1], "dp", down)]
        if self.hops == self.last:
            self.slots[self.hops] = self.ends
        else:
            self.slots[self.hops], self.slots[-self.hops] = [self.ends[0]], [self.ends[1]]


def local(attn_heads, residual, low_hidden, mid_hidden, out_weight, join_weight, join_gain):
    groups, owners = lax.axis_size("dp"), lax.axis_size("tensor")
    tokens, features = attn_heads.shape
    width = out_weight.shape[1]
    xs = owners // 2
    rows = tokens // owners
    ring = ring_of(groups)
    last = groups // 2
    offsets = [0] + [sign * s for s in range(1, last) for sign in (1, -1)] + [last]
    tensor = lax.axis_index("tensor").astype(jnp.uint32)
    core, x = tensor & 1, tensor >> 1

    def swap(values, bit):
        return lax.ppermute(values, "tensor", [(t, t ^ bit) for t in range(owners)])

    def product(slots, weight):
        rows_in = jnp.concatenate([piece for slot in slots for piece in slot], axis=0)
        return jnp.dot(rows_in, weight, preferred_element_type=jnp.float32).reshape(len(slots), tokens, width)

    def bit_of_x(half):
        return (x >> (half.bit_length() - 1)) & 1

    attn = Gather(attn_heads)
    per_owner = groups // owners
    classes = list(reversed(range(per_owner)))
    kept = {kind: [k for k in offsets if k % per_owner == kind] for kind in classes}
    kept = {kind: slots[-1:] + slots[:-1] for kind, slots in kept.items()}
    pair_sums = {kind: [None] * xs for kind in classes}

    parts = {}

    def multiply_slots(slots):
        products = product([attn.slots[k] for k in slots], out_weight)
        parts.update({k: products[n] for n, k in enumerate(slots)})

    def sum_cores(reach):
        ready = []
        for kind in classes:
            for i, pair in enumerate(zip(kept[kind][::2], kept[kind][1::2])):
                if pair_sums[kind][i] is None and max(abs(k) for k in pair) <= reach:
                    ready.append((kind, i, parts[pair[0]], parts[pair[1]]))
        came = swap(jnp.stack([jnp.where(core == 0, second, first) for _, _, first, second in ready]), 1)
        for n, (kind, i, first, second) in enumerate(ready):
            pair_sums[kind][i] = jnp.where(core == 0, first, second) + came[n]

    low = Gather(low_hidden)
    mid = Gather(mid_hidden)
    for hop in range(1, last + 1):
        attn.ends, low.ends, mid.ends, parts = tie(attn.ends, low.ends, mid.ends, parts)
        attn.hop()
        (mid if hop == last else low).hop()
        if hop == 2:
            multiply_slots([0])
        if hop > 1:
            multiply_slots([hop - 1, 1 - hop])
    def sum_xs(parts):
        while len(parts) > 1:
            half = len(parts) // 2
            high = bit_of_x(half) == 1
            sent = jnp.stack([jnp.where(high, a, b) for a, b in zip(parts[:half], parts[half:])]).astype(jnp.bfloat16)
            came = swap(sent, 2 * half)
            parts = [
                jnp.where(high, b, a) + came[i].astype(jnp.float32)
                for i, (a, b) in enumerate(zip(parts[:half], parts[half:]))
            ]
        return parts[0]

    sum_cores(last - 1)
    held = {kind: sum_xs(pair_sums[kind]).astype(jnp.bfloat16) for kind in classes[:-1]}
    attn.slots[last], pair_sums, held = tie(attn.ends, pair_sums, held)
    multiply_slots([last])
    sum_cores(last)
    held[classes[-1]] = sum_xs(pair_sums[classes[-1]]).astype(jnp.bfloat16)
    held[classes[-1]], mid.ends = tie(held[classes[-1]], mid.ends)

    arrived = []
    for kind in classes:
        moves = [
            (d * owners + t, ring[(p - kept[kind][t]) % groups] * owners + d // per_owner)
            for p, d in enumerate(ring)
            for t in range(owners)
        ]
        arrived.append(lax.ppermute(held[kind], ("dp", "tensor"), moves))
    own_top = pl.pallas_call(
        functools.partial(top_body, groups, classes, width),
        out_shape=jax.ShapeDtypeStruct((tokens, features), jnp.bfloat16),
        in_specs=[VMEM] * (len(classes) + 1),
        out_specs=VMEM,
        name="add_residual",
    )(*arrived, residual)

    own_top, mid.ends, mid.slots = tie(own_top, mid.ends, mid.slots)
    top = Gather(own_top)
    chunks = [[s, -s] for s in range(1, last)] + [[last, 0]]
    owned = {}

    def multiply(part, depth, weight):
        return product([depth.slots[k] for k in part], weight)

    def add_cores(total):
        by_owner = total.reshape(total.shape[0], xs, 2, rows, width)
        kept_part = lax.dynamic_index_in_dim(by_owner, core, 2, keepdims=False)
        sent_part = lax.dynamic_index_in_dim(by_owner, 1 - core, 2, keepdims=False)
        return kept_part + swap(sent_part, 1)

    def send(part, k, flip=0):
        if not k and not flip:
            return part
        moves = [
            (ring[q] * owners + t, ring[(q - k) % groups] * owners + (t ^ (2 * flip)))
            for q in range(groups)
            for t in range(owners)
        ]
        return lax.ppermute(part.astype(jnp.bfloat16), ("dp", "tensor"), moves)

    def add_x(total):
        half = xs // 2
        while half:
            total = total.reshape((total.shape[0], 2, half) + total.shape[-2:])
            side = bit_of_x(half)
            sent = lax.dynamic_index_in_dim(total, 1 - side, 1, keepdims=False).astype(jnp.bfloat16)
            total = lax.dynamic_index_in_dim(total, side, 1, keepdims=False) + swap(sent, 2 * half).astype(jnp.float32)
            half //= 2
        return total.reshape(total.shape[0], rows, width)

    def send_all(part, total):
        for i, k in enumerate(part):
            owned[k] = [send(total[i], k)]

    def add_halves(part, total):
        for flip in range(xs):
            for i, k in enumerate(part):
                owned.setdefault(k, []).append(send(pick(total[i], x ^ flip), k, flip))

    def last_hops(*gathers):
        joint = Gather(None)
        joint.hops = last - 1
        joint.halves = lambda: [jnp.concatenate(ends) for ends in zip(*[gather.halves() for gather in gathers])]
        joint.hop()
        for gather, *pieces in zip(gathers, *[jnp.split(end, len(gathers)) for end in joint.ends]):
            gather.slots[last] = pieces

    def multiply_deep(part):
        return multiply(part, low, join_weight[0]) + multiply(part, mid, join_weight[1])

    deep_sum, cored, summed = None, None, None
    for hop in range(1, last + 1):
        top.ends, mid.ends, low.ends, deep_sum, cored = tie(top.ends, mid.ends, low.ends, deep_sum, cored)
        top.hop()
        if hop < last - 1:
            mid.hop()
        elif hop == last - 1:
            last_hops(low, mid)
        if cored is not None:
            summed = add_x(cored)
            if hop < last:
                send_all(chunks[hop - 3], summed)
        if hop > 1:
            cored = add_cores(multiply(chunks[hop - 2], top, join_weight[2]) + deep_sum)
        deep_sum = multiply_deep(chunks[hop - 1])
    top.slots[last], deep_sum, summed = tie(top.ends, deep_sum, summed)
    send_all(chunks[-3], summed)
    send_all(chunks[-2], add_x(cored))
    add_halves(chunks[-1], add_cores(multiply(chunks[-1], top, join_weight[2]) + deep_sum))
    blocks = [part for k in offsets for part in owned[k]]
    counts = [len(owned[k]) for k in offsets]
    return pl.pallas_call(
        functools.partial(norm_body, offsets, counts, width),
        out_shape=jax.ShapeDtypeStruct((rows, groups * width), jnp.bfloat16),
        in_specs=[VMEM] * (len(blocks) + 1),
        out_specs=VMEM,
        name="norm_rows",
    )(*blocks, join_gain.reshape(1, groups * width))


def solution(mesh):
    return jax.shard_map(
        local,
        mesh=mesh,
        in_specs=(
            P("dp", "tensor"),
            P("dp", "tensor"),
            P("dp", "tensor"),
            P("dp", "tensor"),
            P("tensor", "dp"),
            P(None, "tensor", "dp"),
            P(),
        ),
        out_specs=P(("dp", "tensor"), None),
        check_vma=False,
    )
```

```python
import functools

import jax
import jax.numpy as jnp
from jax import lax
from jax.experimental import pallas as pl
from jax.experimental.pallas import tpu as pltpu
from jax.sharding import PartitionSpec as P


def ring_of(groups):
    half = groups // 2
    return [2 * q for q in range(half)] + [2 * q + 1 for q in reversed(range(half))]


def tie(*values):
    flat, tree = jax.tree.flatten(values)
    return jax.tree.unflatten(tree, lax.optimization_barrier(tuple(flat)))


def pick(values, index):
    return lax.dynamic_index_in_dim(values, index, 0, keepdims=False)


def place_on_ring(groups):
    dp = lax.axis_index("dp")
    return jnp.where(lax.rem(dp, 2) == 0, lax.div(dp, 2), groups - 1 - lax.div(dp, 2))


def top_body(groups, classes, width, *refs):
    arrived, rest_ref, top_ref = refs[: len(classes)], refs[-2], refs[-1]
    home = lax.axis_index("tensor") + place_on_ring(groups)
    for kind, piece_ref in zip(classes, arrived):
        j = lax.rem(home + kind, len(classes))
        columns = pl.ds(pl.multiple_of(j * width, width), width)
        total = rest_ref[:, columns].astype(jnp.float32) + piece_ref[...].astype(jnp.float32)
        top_ref[:, columns] = total.astype(jnp.bfloat16)


def norm_body(offsets, counts, width, *refs):
    groups = len(offsets)
    gain_ref, out_ref = refs[-2:]
    place = place_on_ring(groups)
    blocks, total, first = [], 0.0, 0
    for count in counts:
        block = sum(ref[...].astype(jnp.float32) for ref in refs[first : first + count])
        total = total + jnp.sum(block * block, axis=1, keepdims=True)
        blocks.append(block)
        first += count
    inverse_rms = lax.rsqrt(total / (groups * width) + 1e-05)
    for offset, block in zip(offsets, blocks):
        q = lax.rem(place + offset + groups, groups)
        d = jnp.where(q < groups // 2, 2 * q, 2 * (groups - 1 - q) + 1)
        columns = pl.ds(pl.multiple_of(d * width, width), width)
        out_ref[:, columns] = (block * inverse_rms * gain_ref[:, columns]).astype(jnp.bfloat16)


VMEM = pl.BlockSpec(memory_space=pltpu.VMEM)


class Gather:
    def __init__(self, own, axis):
        self.ring = ring_of(lax.axis_size("dp"))
        self.axis, self.last, self.hops = axis, len(self.ring) // 2, 0
        self.ends = [own, own]
        self.slots = {0: [own]}

    def hop(self):
        count = len(self.ring)
        ends = self.ends
        self.hops += 1
        if self.hops == self.last:
            middle = ends[0].shape[self.axis] // 2
            ends = [
                lax.slice_in_dim(ends[0], 0, middle, axis=self.axis),
                lax.slice_in_dim(ends[1], middle, 2 * middle, axis=self.axis),
            ]
        up = [(self.ring[q], self.ring[(q + 1) % count]) for q in range(count)]
        down = [(target, source) for source, target in up]
        self.ends = [lax.ppermute(ends[0], "dp", up), lax.ppermute(ends[1], "dp", down)]
        if self.hops == self.last:
            self.slots[self.hops] = self.ends
        else:
            self.slots[self.hops], self.slots[-self.hops] = [self.ends[0]], [self.ends[1]]


def local(attn_heads, residual, low_hidden, mid_hidden, out_weight, join_weight, join_gain):
    groups, owners = lax.axis_size("dp"), lax.axis_size("tensor")
    tokens, features = attn_heads.shape
    width = out_weight.shape[1]
    xs = owners // 2
    rows = tokens // owners
    ring = ring_of(groups)
    last = groups // 2
    offsets = [0] + [sign * s for s in range(1, last) for sign in (1, -1)] + [last]
    tensor = lax.axis_index("tensor").astype(jnp.uint32)
    core, x = tensor & 1, tensor >> 1

    def swap(values, bit):
        return lax.ppermute(values, "tensor", [(t, t ^ bit) for t in range(owners)])

    def product(slots, weight):
        rows_in = jnp.concatenate([piece for slot in slots for piece in slot], axis=0)
        return jnp.dot(rows_in, weight, preferred_element_type=jnp.float32).reshape(len(slots), tokens, width)

    def bit_of_x(half):
        return (x >> (half.bit_length() - 1)) & 1

    attn = Gather(attn_heads, 0)
    per_owner = groups // owners
    classes = list(reversed(range(per_owner)))
    kept = {kind: [k for k in offsets if k % per_owner == kind] for kind in classes}
    kept = {kind: slots[-1:] + slots[:-1] for kind, slots in kept.items()}
    pair_sums = {kind: [None] * xs for kind in classes}

    def multiply_pairs(reach):
        made = {}
        for kind in classes:
            for i in range(xs):
                pair = kept[kind][2 * i : 2 * i + 2]
                if max(abs(k) for k in pair) == reach:
                    made[kind, i] = product([attn.slots[k] for k in pair], out_weight)
        return made

    def sum_cores(made):
        for (kind, i), products in made.items():
            pair_sums[kind][i] = pick(products, core) + swap(pick(products, 1 - core), 1)

    low = Gather(low_hidden, 0)
    mid = Gather(mid_hidden, 0)
    for hop in range(1, last + 1):
        attn.ends, low.ends, mid.ends, pair_sums = tie(attn.ends, low.ends, mid.ends, pair_sums)
        attn.hop()
        (mid if hop == last else low).hop()
        sum_cores(multiply_pairs(hop - 1))
    attn.slots[last], pair_sums = tie(attn.ends, pair_sums)
    sum_cores(multiply_pairs(last))

    def sum_xs(parts):
        while len(parts) > 1:
            half = len(parts) // 2
            high = bit_of_x(half) == 1
            sent = jnp.stack([jnp.where(high, a, b) for a, b in zip(parts[:half], parts[half:])]).astype(jnp.bfloat16)
            came = swap(sent, 2 * half)
            parts = [
                jnp.where(high, b, a) + came[i].astype(jnp.float32)
                for i, (a, b) in enumerate(zip(parts[:half], parts[half:]))
            ]
        return parts[0]

    arrived = []
    for kind in classes:
        held = sum_xs(pair_sums[kind]).astype(jnp.bfloat16)
        if kind == classes[-1]:
            held, mid.ends = tie(held, mid.ends)
        moves = [
            (d * owners + t, ring[(p - kept[kind][t]) % groups] * owners + d // per_owner)
            for p, d in enumerate(ring)
            for t in range(owners)
        ]
        arrived.append(lax.ppermute(held, ("dp", "tensor"), moves))
    own_top = pl.pallas_call(
        functools.partial(top_body, groups, classes, width),
        out_shape=jax.ShapeDtypeStruct((tokens, features), jnp.bfloat16),
        in_specs=[VMEM] * (len(classes) + 1),
        out_specs=VMEM,
        name="add_residual",
    )(*arrived, residual)

    own_top, low.ends, mid.ends = tie(own_top, low.ends, mid.ends)
    top = Gather(own_top, 0)
    cuts = [0] + list(range(3, groups, 2)) + [groups]
    chunks = [offsets[low_cut:high_cut] for low_cut, high_cut in zip(cuts, cuts[1:])]
    owned = {}

    def multiply_deep(part):
        total = product([low.slots[k] for k in part], join_weight[0])
        return total + product([mid.slots[k] for k in part], join_weight[1])

    def multiply(part, deep_sum):
        return product([top.slots[k] for k in part], join_weight[2]) + deep_sum

    def add_cores(total):
        by_owner = total.reshape(total.shape[0], xs, 2, rows, width)
        kept_part = lax.dynamic_index_in_dim(by_owner, core, 2, keepdims=False)
        sent_part = lax.dynamic_index_in_dim(by_owner, 1 - core, 2, keepdims=False)
        return kept_part + swap(sent_part, 1)

    def send(part, k, flip=0):
        if not k and not flip:
            return part
        moves = [
            (ring[q] * owners + t, ring[(q - k) % groups] * owners + (t ^ (2 * flip)))
            for q in range(groups)
            for t in range(owners)
        ]
        return lax.ppermute(part.astype(jnp.bfloat16), ("dp", "tensor"), moves)

    def add_x(total, dtype):
        half = xs // 2
        while half:
            total = total.reshape((total.shape[0], 2, half) + total.shape[-2:])
            side = bit_of_x(half)
            sent = lax.dynamic_index_in_dim(total, 1 - side, 1, keepdims=False).astype(dtype)
            total = lax.dynamic_index_in_dim(total, side, 1, keepdims=False) + swap(sent, 2 * half).astype(jnp.float32)
            half //= 2
        return total.reshape(total.shape[0], rows, width)

    def send_all(part, total):
        for i, k in enumerate(part):
            owned[k] = [send(total[i], k)]

    def add_halves(part, total):
        for flip in range(xs):
            for i, k in enumerate(part):
                owned.setdefault(k, []).append(send(pick(total[i], x ^ flip), k, flip))

    cored, deep_sum, summed = None, None, None
    for hop in range(1, last + 1):
        top.ends, mid.ends, low.ends, cored, deep_sum = tie(top.ends, mid.ends, low.ends, cored, deep_sum)
        if hop == 2:
            low.slots[last] = low.ends
        top.hop()
        if mid.hops < last:
            mid.hop()
        if hop == 1:
            low.hop()
        if hop > 2:
            summed = add_x(cored, jnp.float32 if hop == 3 else jnp.bfloat16)
            if hop < last:
                send_all(chunks[hop - 3], summed)
        if hop > 1:
            cored = add_cores(multiply(chunks[hop - 2], deep_sum))
        deep_sum = multiply_deep(chunks[hop - 1])
    top.slots[last], deep_sum, owned, summed = tie(top.ends, deep_sum, owned, summed)
    send_all(chunks[-3], summed)
    send_all(chunks[-2], add_x(cored, jnp.bfloat16))
    add_halves(chunks[-1], add_cores(multiply(chunks[-1], deep_sum)))
    parts = [part for k in offsets for part in owned[k]]
    counts = [len(owned[k]) for k in offsets]
    return pl.pallas_call(
        functools.partial(norm_body, offsets, counts, width),
        out_shape=jax.ShapeDtypeStruct((rows, groups * width), jnp.bfloat16),
        in_specs=[VMEM] * (len(parts) + 1),
        out_specs=VMEM,
        name="norm_rows",
    )(*parts, join_gain.reshape(1, groups * width))


def solution(mesh):
    return jax.shard_map(
        local,
        mesh=mesh,
        in_specs=(
            P("dp", "tensor"),
            P("dp", "tensor"),
            P("dp", "tensor"),
            P("dp", "tensor"),
            P("tensor", "dp"),
            P(None, "tensor", "dp"),
            P(),
        ),
        out_specs=P(("dp", "tensor"), None),
        check_vma=False,
    )
```

```python
import functools

import jax
import jax.numpy as jnp
from jax import lax
from jax.experimental import pallas as pl
from jax.experimental.pallas import tpu as pltpu
from jax.sharding import PartitionSpec as P


def ring_of(groups):
    half = groups // 2
    return [2 * q for q in range(half)] + [2 * q + 1 for q in reversed(range(half))]


def tie(*values):
    flat, tree = jax.tree.flatten(values)
    return jax.tree.unflatten(tree, lax.optimization_barrier(tuple(flat)))


def pick(values, index):
    return lax.dynamic_index_in_dim(values, index, 0, keepdims=False)


def place_on_ring(groups):
    dp = lax.axis_index("dp")
    return jnp.where(lax.rem(dp, 2) == 0, lax.div(dp, 2), groups - 1 - lax.div(dp, 2))


def top_body(groups, classes, width, *refs):
    arrived, rest_ref, top_ref = refs[: len(classes)], refs[-2], refs[-1]
    home = lax.axis_index("tensor") + place_on_ring(groups)
    for kind, piece_ref in zip(classes, arrived):
        j = lax.rem(home + kind, len(classes))
        columns = pl.ds(pl.multiple_of(j * width, width), width)
        total = rest_ref[:, columns].astype(jnp.float32) + piece_ref[...].astype(jnp.float32)
        top_ref[:, columns] = total.astype(jnp.bfloat16)


def norm_body(offsets, counts, width, *refs):
    groups = len(offsets)
    gain_ref, out_ref = refs[-2:]
    place = place_on_ring(groups)
    blocks, total, first = [], 0.0, 0
    for count in counts:
        block = sum(ref[...].astype(jnp.float32) for ref in refs[first : first + count])
        total = total + jnp.sum(block * block, axis=1, keepdims=True)
        blocks.append(block)
        first += count
    inverse_rms = lax.rsqrt(total / (groups * width) + 1e-05)
    for offset, block in zip(offsets, blocks):
        q = lax.rem(place + offset + groups, groups)
        d = jnp.where(q < groups // 2, 2 * q, 2 * (groups - 1 - q) + 1)
        columns = pl.ds(pl.multiple_of(d * width, width), width)
        out_ref[:, columns] = (block * inverse_rms * gain_ref[:, columns]).astype(jnp.bfloat16)


VMEM = pl.BlockSpec(memory_space=pltpu.VMEM)


class Gather:
    def __init__(self, own, axis):
        self.ring = ring_of(lax.axis_size("dp"))
        self.axis, self.last, self.hops = axis, len(self.ring) // 2, 0
        self.ends = [own, own]
        self.slots = {0: [own]}

    def hop(self):
        count = len(self.ring)
        ends = self.ends
        self.hops += 1
        if self.hops == self.last:
            middle = ends[0].shape[self.axis] // 2
            ends = [
                lax.slice_in_dim(ends[0], 0, middle, axis=self.axis),
                lax.slice_in_dim(ends[1], middle, 2 * middle, axis=self.axis),
            ]
        up = [(self.ring[q], self.ring[(q + 1) % count]) for q in range(count)]
        down = [(target, source) for source, target in up]
        self.ends = [lax.ppermute(ends[0], "dp", up), lax.ppermute(ends[1], "dp", down)]
        if self.hops == self.last:
            self.slots[self.hops] = self.ends
        else:
            self.slots[self.hops], self.slots[-self.hops] = [self.ends[0]], [self.ends[1]]


def local(attn_heads, residual, low_hidden, mid_hidden, out_weight, join_weight, join_gain):
    groups, owners = lax.axis_size("dp"), lax.axis_size("tensor")
    tokens, features = attn_heads.shape
    width = out_weight.shape[1]
    xs = owners // 2
    rows = tokens // owners
    ring = ring_of(groups)
    last = groups // 2
    offsets = [0] + [sign * s for s in range(1, last) for sign in (1, -1)] + [last]
    tensor = lax.axis_index("tensor").astype(jnp.uint32)
    core, x = tensor & 1, tensor >> 1

    def swap(values, bit):
        return lax.ppermute(values, "tensor", [(t, t ^ bit) for t in range(owners)])

    def product(slots, weight):
        rows_in = jnp.concatenate([piece for slot in slots for piece in slot], axis=0)
        return jnp.dot(rows_in, weight, preferred_element_type=jnp.float32).reshape(len(slots), tokens, width)

    def bit_of_x(half):
        return (x >> (half.bit_length() - 1)) & 1

    attn = Gather(attn_heads, 0)
    per_owner = groups // owners
    classes = list(reversed(range(per_owner)))
    kept = {kind: [k for k in offsets if k % per_owner == kind] for kind in classes}
    kept = {kind: slots[-1:] + slots[:-1] for kind, slots in kept.items()}
    pair_sums = {kind: [None] * xs for kind in classes}

    def multiply_pairs(reach):
        made = {}
        for kind in classes:
            for i in range(xs):
                pair = kept[kind][2 * i : 2 * i + 2]
                if max(abs(k) for k in pair) == reach:
                    made[kind, i] = product([attn.slots[k] for k in pair], out_weight)
        return made

    def sum_cores(made):
        for (kind, i), products in made.items():
            pair_sums[kind][i] = pick(products, core) + swap(pick(products, 1 - core), 1)

    low = Gather(low_hidden, 0)
    mid = Gather(mid_hidden, 0)
    for hop in range(1, last + 1):
        attn.ends, low.ends, mid.ends, pair_sums = tie(attn.ends, low.ends, mid.ends, pair_sums)
        attn.hop()
        (mid if hop == last else low).hop()
        sum_cores(multiply_pairs(hop - 1))
    low.ends, attn.ends = tie(low.ends, attn.ends)
    low.hop()
    attn.slots[last], pair_sums = tie(attn.ends, pair_sums)
    sum_cores(multiply_pairs(last))

    def sum_xs(parts):
        while len(parts) > 1:
            half = len(parts) // 2
            high = bit_of_x(half) == 1
            sent = jnp.stack([jnp.where(high, a, b) for a, b in zip(parts[:half], parts[half:])]).astype(jnp.bfloat16)
            came = swap(sent, 2 * half)
            parts = [
                jnp.where(high, b, a) + came[i].astype(jnp.float32)
                for i, (a, b) in enumerate(zip(parts[:half], parts[half:]))
            ]
        return parts[0]

    arrived = []
    for kind in classes:
        held = sum_xs(pair_sums[kind]).astype(jnp.bfloat16)
        if kind == classes[-1]:
            held, mid.ends = tie(held, mid.ends)
        moves = [
            (d * owners + t, ring[(p - kept[kind][t]) % groups] * owners + d // per_owner)
            for p, d in enumerate(ring)
            for t in range(owners)
        ]
        arrived.append(lax.ppermute(held, ("dp", "tensor"), moves))
    own_top = pl.pallas_call(
        functools.partial(top_body, groups, classes, width),
        out_shape=jax.ShapeDtypeStruct((tokens, features), jnp.bfloat16),
        in_specs=[VMEM] * (len(classes) + 1),
        out_specs=VMEM,
        name="add_residual",
    )(*arrived, residual)

    own_top, low.slots[last] = tie(own_top, low.slots[last])
    top = Gather(own_top, 0)
    cuts = [0] + list(range(3, groups, 2)) + [groups]
    chunks = [offsets[low_cut:high_cut] for low_cut, high_cut in zip(cuts, cuts[1:])]
    owned = {}

    def multiply_deep(part):
        total = product([low.slots[k] for k in part], join_weight[0])
        return total + product([mid.slots[k] for k in part], join_weight[1])

    def multiply(part, deep_sum):
        return product([top.slots[k] for k in part], join_weight[2]) + deep_sum

    def add_cores(total):
        by_owner = total.reshape(total.shape[0], xs, 2, rows, width)
        kept_part = lax.dynamic_index_in_dim(by_owner, core, 2, keepdims=False)
        sent_part = lax.dynamic_index_in_dim(by_owner, 1 - core, 2, keepdims=False)
        return kept_part + swap(sent_part, 1)

    def send(part, k, flip=0):
        if not k and not flip:
            return part
        moves = [
            (ring[q] * owners + t, ring[(q - k) % groups] * owners + (t ^ (2 * flip)))
            for q in range(groups)
            for t in range(owners)
        ]
        return lax.ppermute(part.astype(jnp.bfloat16), ("dp", "tensor"), moves)

    def add_x(total):
        half = xs // 2
        while half:
            total = total.reshape((total.shape[0], 2, half) + total.shape[-2:])
            side = bit_of_x(half)
            sent = lax.dynamic_index_in_dim(total, 1 - side, 1, keepdims=False).astype(jnp.bfloat16)
            total = lax.dynamic_index_in_dim(total, side, 1, keepdims=False) + swap(sent, 2 * half).astype(jnp.float32)
            half //= 2
        return total.reshape(total.shape[0], rows, width)

    def send_all(part, total):
        for i, k in enumerate(part):
            owned[k] = [send(total[i], k)]

    def add_halves(part, total):
        for flip in range(xs):
            for i, k in enumerate(part):
                owned.setdefault(k, []).append(send(pick(total[i], x ^ flip), k, flip))

    cored, deep_sum, summed = None, None, None
    for hop in range(1, last + 1):
        if hop < last:
            top.ends, mid.ends, cored, deep_sum = tie(top.ends, mid.ends, cored, deep_sum)
        else:
            top.ends, cored, deep_sum = tie(top.ends, cored, deep_sum)
        top.hop()
        if hop < last - 1:
            mid.hop()
        if hop > 2:
            summed = add_x(cored)
            if hop == last - 1:
                mid.ends, summed = tie(mid.ends, summed)
                mid.hop()
            if hop < last:
                send_all(chunks[hop - 3], summed)
        if hop > 1:
            cored = add_cores(multiply(chunks[hop - 2], deep_sum))
        if hop < last:
            deep_sum = multiply_deep(chunks[hop - 1])
    deep_sum = multiply_deep(chunks[-1])
    top.slots[last], deep_sum, owned, summed = tie(top.ends, deep_sum, owned, summed)
    send_all(chunks[-3], summed)
    send_all(chunks[-2], add_x(cored))
    add_halves(chunks[-1], add_cores(multiply(chunks[-1], deep_sum)))
    parts = [part for k in offsets for part in owned[k]]
    counts = [len(owned[k]) for k in offsets]
    return pl.pallas_call(
        functools.partial(norm_body, offsets, counts, width),
        out_shape=jax.ShapeDtypeStruct((rows, groups * width), jnp.bfloat16),
        in_specs=[VMEM] * (len(parts) + 1),
        out_specs=VMEM,
        name="norm_rows",
    )(*parts, join_gain.reshape(1, groups * width))


def solution(mesh):
    return jax.shard_map(
        local,
        mesh=mesh,
        in_specs=(
            P("dp", "tensor"),
            P("dp", "tensor"),
            P("dp", "tensor"),
            P("dp", "tensor"),
            P("tensor", "dp"),
            P(None, "tensor", "dp"),
            P(),
        ),
        out_specs=P(("dp", "tensor"), None),
        check_vma=False,
    )
```

```python
import functools

import jax
import jax.numpy as jnp
from jax import lax
from jax.experimental import pallas as pl
from jax.experimental.pallas import tpu as pltpu
from jax.sharding import PartitionSpec as P


def ring_of(groups):
    half = groups // 2
    return [2 * q for q in range(half)] + [2 * q + 1 for q in reversed(range(half))]


def tie(*values):
    flat, tree = jax.tree.flatten(values)
    return jax.tree.unflatten(tree, lax.optimization_barrier(tuple(flat)))


def pick(values, index):
    return lax.dynamic_index_in_dim(values, index, 0, keepdims=False)


def place_on_ring(groups):
    dp = lax.axis_index("dp")
    return jnp.where(lax.rem(dp, 2) == 0, lax.div(dp, 2), groups - 1 - lax.div(dp, 2))


def top_body(groups, classes, width, *refs):
    arrived, rest_ref, top_ref = refs[: len(classes)], refs[-2], refs[-1]
    home = lax.axis_index("tensor") + place_on_ring(groups)
    for kind, piece_ref in zip(classes, arrived):
        j = lax.rem(home + kind, len(classes))
        columns = pl.ds(pl.multiple_of(j * width, width), width)
        total = rest_ref[:, columns].astype(jnp.float32) + piece_ref[...].astype(jnp.float32)
        top_ref[:, columns] = total.astype(jnp.bfloat16)


def norm_body(offsets, counts, width, *refs):
    groups = len(offsets)
    gain_ref, out_ref = refs[-2:]
    place = place_on_ring(groups)
    blocks, total, first = [], 0.0, 0
    for count in counts:
        block = sum(ref[...].astype(jnp.float32) for ref in refs[first : first + count])
        total = total + jnp.sum(block * block, axis=1, keepdims=True)
        blocks.append(block)
        first += count
    inverse_rms = lax.rsqrt(total / (groups * width) + 1e-05)
    for offset, block in zip(offsets, blocks):
        q = lax.rem(place + offset + groups, groups)
        d = jnp.where(q < groups // 2, 2 * q, 2 * (groups - 1 - q) + 1)
        columns = pl.ds(pl.multiple_of(d * width, width), width)
        out_ref[:, columns] = (block * inverse_rms * gain_ref[:, columns]).astype(jnp.bfloat16)


VMEM = pl.BlockSpec(memory_space=pltpu.VMEM)


class Gather:
    def __init__(self, own, axis):
        self.ring = ring_of(lax.axis_size("dp"))
        self.axis, self.last, self.hops = axis, len(self.ring) // 2, 0
        self.ends = [own, own]
        self.slots = {0: [own]}

    def hop(self):
        count = len(self.ring)
        ends = self.ends
        self.hops += 1
        if self.hops == self.last:
            middle = ends[0].shape[self.axis] // 2
            ends = [
                lax.slice_in_dim(ends[0], 0, middle, axis=self.axis),
                lax.slice_in_dim(ends[1], middle, 2 * middle, axis=self.axis),
            ]
        up = [(self.ring[q], self.ring[(q + 1) % count]) for q in range(count)]
        down = [(target, source) for source, target in up]
        self.ends = [lax.ppermute(ends[0], "dp", up), lax.ppermute(ends[1], "dp", down)]
        if self.hops == self.last:
            self.slots[self.hops] = self.ends
        else:
            self.slots[self.hops], self.slots[-self.hops] = [self.ends[0]], [self.ends[1]]


def local(attn_heads, residual, low_hidden, mid_hidden, out_weight, join_weight, join_gain):
    groups, owners = lax.axis_size("dp"), lax.axis_size("tensor")
    tokens, features = attn_heads.shape
    width = out_weight.shape[1]
    xs = owners // 2
    rows = tokens // owners
    ring = ring_of(groups)
    last = groups // 2
    offsets = [0] + [sign * s for s in range(1, last) for sign in (1, -1)] + [last]
    tensor = lax.axis_index("tensor").astype(jnp.uint32)
    core, x = tensor & 1, tensor >> 1

    def swap(values, bit):
        return lax.ppermute(values, "tensor", [(t, t ^ bit) for t in range(owners)])

    def product(slots, weight):
        rows_in = jnp.concatenate([piece for slot in slots for piece in slot], axis=0)
        return jnp.dot(rows_in, weight, preferred_element_type=jnp.float32).reshape(len(slots), tokens, width)

    def bit_of_x(half):
        return (x >> (half.bit_length() - 1)) & 1

    attn = Gather(attn_heads, 0)
    per_owner = groups // owners
    classes = list(reversed(range(per_owner)))
    kept = {kind: [k for k in offsets if k % per_owner == kind] for kind in classes}
    kept = {kind: slots[-1:] + slots[:-1] for kind, slots in kept.items()}
    pair_sums = {kind: [None] * xs for kind in classes}

    def multiply_pairs(reach):
        made = {}
        for kind in classes:
            for i in range(xs):
                pair = kept[kind][2 * i : 2 * i + 2]
                if max(abs(k) for k in pair) == reach:
                    made[kind, i] = product([attn.slots[k] for k in pair], out_weight)
        return made

    def sum_cores(made):
        for (kind, i), products in made.items():
            pair_sums[kind][i] = pick(products, core) + swap(pick(products, 1 - core), 1)

    low = Gather(low_hidden, 0)
    mid = Gather(mid_hidden, 0)
    for hop in range(1, last + 1):
        attn.ends, low.ends, mid.ends, pair_sums = tie(attn.ends, low.ends, mid.ends, pair_sums)
        attn.hop()
        (mid if hop == last else low).hop()
        sum_cores(multiply_pairs(hop - 1))
    attn.slots[last], pair_sums = tie(attn.ends, pair_sums)
    sum_cores(multiply_pairs(last))

    def sum_xs(parts):
        while len(parts) > 1:
            half = len(parts) // 2
            high = bit_of_x(half) == 1
            sent = jnp.stack([jnp.where(high, a, b) for a, b in zip(parts[:half], parts[half:])]).astype(jnp.bfloat16)
            came = swap(sent, 2 * half)
            parts = [
                jnp.where(high, b, a) + came[i].astype(jnp.float32)
                for i, (a, b) in enumerate(zip(parts[:half], parts[half:]))
            ]
        return parts[0]

    arrived = []
    for kind in classes:
        held = sum_xs(pair_sums[kind]).astype(jnp.bfloat16)
        if kind == classes[-1]:
            held, mid.ends, low.ends = tie(held, mid.ends, low.ends)
            low.hop()
        moves = [
            (d * owners + t, ring[(p - kept[kind][t]) % groups] * owners + d // per_owner)
            for p, d in enumerate(ring)
            for t in range(owners)
        ]
        arrived.append(lax.ppermute(held, ("dp", "tensor"), moves))
    own_top = pl.pallas_call(
        functools.partial(top_body, groups, classes, width),
        out_shape=jax.ShapeDtypeStruct((tokens, features), jnp.bfloat16),
        in_specs=[VMEM] * (len(classes) + 1),
        out_specs=VMEM,
        name="add_residual",
    )(*arrived, residual)

    own_top, low.slots[last] = tie(own_top, low.slots[last])
    top = Gather(own_top, 0)
    cuts = [0] + list(range(3, groups, 2)) + [groups]
    chunks = [offsets[low_cut:high_cut] for low_cut, high_cut in zip(cuts, cuts[1:])]
    owned = {}

    def multiply_deep(part):
        total = product([low.slots[k] for k in part], join_weight[0])
        return total + product([mid.slots[k] for k in part], join_weight[1])

    def multiply(part, deep_sum):
        return product([top.slots[k] for k in part], join_weight[2]) + deep_sum

    def add_cores(total):
        by_owner = total.reshape(total.shape[0], xs, 2, rows, width)
        kept_part = lax.dynamic_index_in_dim(by_owner, core, 2, keepdims=False)
        sent_part = lax.dynamic_index_in_dim(by_owner, 1 - core, 2, keepdims=False)
        return kept_part + swap(sent_part, 1)

    def send(part, k, flip=0):
        if not k and not flip:
            return part
        moves = [
            (ring[q] * owners + t, ring[(q - k) % groups] * owners + (t ^ (2 * flip)))
            for q in range(groups)
            for t in range(owners)
        ]
        return lax.ppermute(part.astype(jnp.bfloat16), ("dp", "tensor"), moves)

    def add_x(total):
        half = xs // 2
        while half:
            total = total.reshape((total.shape[0], 2, half) + total.shape[-2:])
            side = bit_of_x(half)
            sent = lax.dynamic_index_in_dim(total, 1 - side, 1, keepdims=False).astype(jnp.bfloat16)
            total = lax.dynamic_index_in_dim(total, side, 1, keepdims=False) + swap(sent, 2 * half).astype(jnp.float32)
            half //= 2
        return total.reshape(total.shape[0], rows, width)

    def send_all(part, total):
        for i, k in enumerate(part):
            owned[k] = [send(total[i], k)]

    def add_halves(part, total):
        for flip in range(xs):
            for i, k in enumerate(part):
                owned.setdefault(k, []).append(send(pick(total[i], x ^ flip), k, flip))

    cored, deep_sum, summed = None, None, None
    for hop in range(1, last + 1):
        if hop < last:
            top.ends, mid.ends, cored, deep_sum = tie(top.ends, mid.ends, cored, deep_sum)
        else:
            top.ends, cored, deep_sum = tie(top.ends, cored, deep_sum)
        top.hop()
        if hop < last - 1:
            mid.hop()
        if hop > 2:
            summed = add_x(cored)
            if hop == last - 1:
                mid.ends, summed = tie(mid.ends, summed)
                mid.hop()
            if hop < last:
                send_all(chunks[hop - 3], summed)
        if hop > 1:
            cored = add_cores(multiply(chunks[hop - 2], deep_sum))
        if hop < last:
            deep_sum = multiply_deep(chunks[hop - 1])
    deep_sum = multiply_deep(chunks[-1])
    top.slots[last], deep_sum, owned, summed = tie(top.ends, deep_sum, owned, summed)
    send_all(chunks[-3], summed)
    send_all(chunks[-2], add_x(cored))
    add_halves(chunks[-1], add_cores(multiply(chunks[-1], deep_sum)))
    parts = [part for k in offsets for part in owned[k]]
    counts = [len(owned[k]) for k in offsets]
    return pl.pallas_call(
        functools.partial(norm_body, offsets, counts, width),
        out_shape=jax.ShapeDtypeStruct((rows, groups * width), jnp.bfloat16),
        in_specs=[VMEM] * (len(parts) + 1),
        out_specs=VMEM,
        name="norm_rows",
    )(*parts, join_gain.reshape(1, groups * width))


def solution(mesh):
    return jax.shard_map(
        local,
        mesh=mesh,
        in_specs=(
            P("dp", "tensor"),
            P("dp", "tensor"),
            P("dp", "tensor"),
            P("dp", "tensor"),
            P("tensor", "dp"),
            P(None, "tensor", "dp"),
            P(),
        ),
        out_specs=P(("dp", "tensor"), None),
        check_vma=False,
    )
```

```python
import functools

import jax
import jax.numpy as jnp
from jax import lax
from jax.experimental import pallas as pl
from jax.experimental.pallas import tpu as pltpu
from jax.sharding import PartitionSpec as P


def ring_of(groups):
    half = groups // 2
    return [2 * q for q in range(half)] + [2 * q + 1 for q in reversed(range(half))]


def tie(*values):
    flat, tree = jax.tree.flatten(values)
    return jax.tree.unflatten(tree, lax.optimization_barrier(tuple(flat)))


def pick(values, index):
    return lax.dynamic_index_in_dim(values, index, 0, keepdims=False)


def place_on_ring(groups):
    dp = lax.axis_index("dp")
    return jnp.where(lax.rem(dp, 2) == 0, lax.div(dp, 2), groups - 1 - lax.div(dp, 2))


def top_body(groups, classes, width, *refs):
    arrived, rest_ref, top_ref = refs[: len(classes)], refs[-2], refs[-1]
    home = lax.axis_index("tensor") + place_on_ring(groups)
    for kind, piece_ref in zip(classes, arrived):
        j = lax.rem(home + kind, len(classes))
        columns = pl.ds(pl.multiple_of(j * width, width), width)
        total = rest_ref[:, columns].astype(jnp.float32) + piece_ref[...].astype(jnp.float32)
        top_ref[:, columns] = total.astype(jnp.bfloat16)


def norm_body(offsets, counts, width, *refs):
    groups = len(offsets)
    gain_ref, out_ref = refs[-2:]
    place = place_on_ring(groups)
    blocks, total, first = [], 0.0, 0
    for count in counts:
        block = sum(ref[...].astype(jnp.float32) for ref in refs[first : first + count])
        total = total + jnp.sum(block * block, axis=1, keepdims=True)
        blocks.append(block)
        first += count
    inverse_rms = lax.rsqrt(total / (groups * width) + 1e-05)
    for offset, block in zip(offsets, blocks):
        q = lax.rem(place + offset + groups, groups)
        d = jnp.where(q < groups // 2, 2 * q, 2 * (groups - 1 - q) + 1)
        columns = pl.ds(pl.multiple_of(d * width, width), width)
        out_ref[:, columns] = (block * inverse_rms * gain_ref[:, columns]).astype(jnp.bfloat16)


VMEM = pl.BlockSpec(memory_space=pltpu.VMEM)


class Gather:
    def __init__(self, own, axis):
        self.ring = ring_of(lax.axis_size("dp"))
        self.axis, self.last, self.hops = axis, len(self.ring) // 2, 0
        self.ends = [own, own]
        self.slots = {0: [own]}

    def hop(self):
        count = len(self.ring)
        ends = self.ends
        self.hops += 1
        if self.hops == self.last:
            middle = ends[0].shape[self.axis] // 2
            ends = [
                lax.slice_in_dim(ends[0], 0, middle, axis=self.axis),
                lax.slice_in_dim(ends[1], middle, 2 * middle, axis=self.axis),
            ]
        up = [(self.ring[q], self.ring[(q + 1) % count]) for q in range(count)]
        down = [(target, source) for source, target in up]
        self.ends = [lax.ppermute(ends[0], "dp", up), lax.ppermute(ends[1], "dp", down)]
        if self.hops == self.last:
            self.slots[self.hops] = self.ends
        else:
            self.slots[self.hops], self.slots[-self.hops] = [self.ends[0]], [self.ends[1]]


def local(attn_heads, residual, low_hidden, mid_hidden, out_weight, join_weight, join_gain):
    groups, owners = lax.axis_size("dp"), lax.axis_size("tensor")
    tokens, features = attn_heads.shape
    width = out_weight.shape[1]
    xs = owners // 2
    rows = tokens // owners
    ring = ring_of(groups)
    last = groups // 2
    offsets = [0] + [sign * s for s in range(1, last) for sign in (1, -1)] + [last]
    tensor = lax.axis_index("tensor").astype(jnp.uint32)
    core, x = tensor & 1, tensor >> 1

    def swap(values, bit):
        return lax.ppermute(values, "tensor", [(t, t ^ bit) for t in range(owners)])

    def product(slots, weight):
        rows_in = jnp.concatenate([piece for slot in slots for piece in slot], axis=0)
        return jnp.dot(rows_in, weight, preferred_element_type=jnp.float32).reshape(len(slots), tokens, width)

    def bit_of_x(half):
        return (x >> (half.bit_length() - 1)) & 1

    attn = Gather(attn_heads, 0)
    per_owner = groups // owners
    classes = list(reversed(range(per_owner)))
    kept = {kind: [k for k in offsets if k % per_owner == kind] for kind in classes}
    kept = {kind: slots[-1:] + slots[:-1] for kind, slots in kept.items()}
    pair_sums = {kind: [None] * xs for kind in classes}

    def multiply_pairs(reach):
        made = {}
        for kind in classes:
            for i in range(xs):
                pair = kept[kind][2 * i : 2 * i + 2]
                if max(abs(k) for k in pair) == reach:
                    made[kind, i] = product([attn.slots[k] for k in pair], out_weight)
        return made

    def sum_cores(made):
        for (kind, i), products in made.items():
            pair_sums[kind][i] = pick(products, core) + swap(pick(products, 1 - core), 1)

    low = Gather(low_hidden, 0)
    mid = Gather(mid_hidden, 0)
    first_low = None
    for hop in range(1, last + 1):
        attn.ends, low.ends, mid.ends, pair_sums, first_low = tie(attn.ends, low.ends, mid.ends, pair_sums, first_low)
        attn.hop()
        (mid if hop == last else low).hop()
        if hop == 2:
            first_low = product([low.slots[k] for k in offsets[:3]], join_weight[0])
        sum_cores(multiply_pairs(hop - 1))
    attn.slots[last], pair_sums = tie(attn.ends, pair_sums)
    sum_cores(multiply_pairs(last))

    def sum_xs(parts):
        while len(parts) > 1:
            half = len(parts) // 2
            high = bit_of_x(half) == 1
            sent = jnp.stack([jnp.where(high, a, b) for a, b in zip(parts[:half], parts[half:])]).astype(jnp.bfloat16)
            came = swap(sent, 2 * half)
            parts = [
                jnp.where(high, b, a) + came[i].astype(jnp.float32)
                for i, (a, b) in enumerate(zip(parts[:half], parts[half:]))
            ]
        return parts[0]

    arrived = []
    for kind in classes:
        held = sum_xs(pair_sums[kind]).astype(jnp.bfloat16)
        if kind == classes[-1]:
            held, mid.ends, low.ends = tie(held, mid.ends, low.ends)
            low.hop()
        moves = [
            (d * owners + t, ring[(p - kept[kind][t]) % groups] * owners + d // per_owner)
            for p, d in enumerate(ring)
            for t in range(owners)
        ]
        arrived.append(lax.ppermute(held, ("dp", "tensor"), moves))
    own_top = pl.pallas_call(
        functools.partial(top_body, groups, classes, width),
        out_shape=jax.ShapeDtypeStruct((tokens, features), jnp.bfloat16),
        in_specs=[VMEM] * (len(classes) + 1),
        out_specs=VMEM,
        name="add_residual",
    )(*arrived, residual)

    own_top, low.slots[last] = tie(own_top, low.slots[last])
    top = Gather(own_top, 0)
    cuts = [0] + list(range(3, groups, 2)) + [groups]
    chunks = [offsets[low_cut:high_cut] for low_cut, high_cut in zip(cuts, cuts[1:])]
    owned = {}

    def multiply_deep(part):
        total = first_low if part == chunks[0] else product([low.slots[k] for k in part], join_weight[0])
        return total + product([mid.slots[k] for k in part], join_weight[1])

    def multiply(part, deep_sum):
        return product([top.slots[k] for k in part], join_weight[2]) + deep_sum

    def add_cores(total):
        by_owner = total.reshape(total.shape[0], xs, 2, rows, width)
        kept_part = lax.dynamic_index_in_dim(by_owner, core, 2, keepdims=False)
        sent_part = lax.dynamic_index_in_dim(by_owner, 1 - core, 2, keepdims=False)
        return kept_part + swap(sent_part, 1)

    def send(part, k, flip=0):
        if not k and not flip:
            return part
        moves = [
            (ring[q] * owners + t, ring[(q - k) % groups] * owners + (t ^ (2 * flip)))
            for q in range(groups)
            for t in range(owners)
        ]
        return lax.ppermute(part.astype(jnp.bfloat16), ("dp", "tensor"), moves)

    def add_x(total):
        half = xs // 2
        while half:
            total = total.reshape((total.shape[0], 2, half) + total.shape[-2:])
            side = bit_of_x(half)
            sent = lax.dynamic_index_in_dim(total, 1 - side, 1, keepdims=False).astype(jnp.bfloat16)
            total = lax.dynamic_index_in_dim(total, side, 1, keepdims=False) + swap(sent, 2 * half).astype(jnp.float32)
            half //= 2
        return total.reshape(total.shape[0], rows, width)

    def send_all(part, total):
        for i, k in enumerate(part):
            owned[k] = [send(total[i], k)]

    def add_halves(part, total):
        for flip in range(xs):
            for i, k in enumerate(part):
                owned.setdefault(k, []).append(send(pick(total[i], x ^ flip), k, flip))

    cored, deep_sum, summed = None, None, None
    for hop in range(1, last + 1):
        if hop < last:
            top.ends, mid.ends, cored, deep_sum = tie(top.ends, mid.ends, cored, deep_sum)
        else:
            top.ends, cored, deep_sum = tie(top.ends, cored, deep_sum)
        top.hop()
        if hop < last - 1:
            mid.hop()
        if hop > 2:
            summed = add_x(cored)
            if hop == last:
                mid.ends, summed = tie(mid.ends, summed)
                mid.hop()
            if hop < last:
                send_all(chunks[hop - 3], summed)
        if hop > 1:
            cored = add_cores(multiply(chunks[hop - 2], deep_sum))
        if hop < last:
            deep_sum = multiply_deep(chunks[hop - 1])
    deep_sum = multiply_deep(chunks[-1])
    top.slots[last], owned, summed = tie(top.ends, owned, summed)
    send_all(chunks[-3], summed)
    send_all(chunks[-2], add_x(cored))
    add_halves(chunks[-1], add_cores(multiply(chunks[-1], deep_sum)))
    parts = [part for k in offsets for part in owned[k]]
    counts = [len(owned[k]) for k in offsets]
    return pl.pallas_call(
        functools.partial(norm_body, offsets, counts, width),
        out_shape=jax.ShapeDtypeStruct((rows, groups * width), jnp.bfloat16),
        in_specs=[VMEM] * (len(parts) + 1),
        out_specs=VMEM,
        name="norm_rows",
    )(*parts, join_gain.reshape(1, groups * width))


def solution(mesh):
    return jax.shard_map(
        local,
        mesh=mesh,
        in_specs=(
            P("dp", "tensor"),
            P("dp", "tensor"),
            P("dp", "tensor"),
            P("dp", "tensor"),
            P("tensor", "dp"),
            P(None, "tensor", "dp"),
            P(),
        ),
        out_specs=P(("dp", "tensor"), None),
        check_vma=False,
    )
```

```python
import functools

import jax
import jax.numpy as jnp
from jax import lax
from jax.experimental import pallas as pl
from jax.experimental.pallas import tpu as pltpu
from jax.sharding import PartitionSpec as P


def ring_of(groups):
    half = groups // 2
    return [2 * q for q in range(half)] + [2 * q + 1 for q in reversed(range(half))]


def tie(*values):
    flat, tree = jax.tree.flatten(values)
    return jax.tree.unflatten(tree, lax.optimization_barrier(tuple(flat)))


def pick(values, index):
    return lax.dynamic_index_in_dim(values, index, 0, keepdims=False)


def place_on_ring(groups):
    dp = lax.axis_index("dp")
    return jnp.where(lax.rem(dp, 2) == 0, lax.div(dp, 2), groups - 1 - lax.div(dp, 2))


def top_body(groups, classes, width, *refs):
    arrived, rest_ref, top_ref = refs[: len(classes)], refs[-2], refs[-1]
    home = lax.axis_index("tensor") + place_on_ring(groups)
    for kind, piece_ref in zip(classes, arrived):
        j = lax.rem(home + kind, len(classes))
        columns = pl.ds(pl.multiple_of(j * width, width), width)
        total = rest_ref[:, columns].astype(jnp.float32) + piece_ref[...].astype(jnp.float32)
        top_ref[:, columns] = total.astype(jnp.bfloat16)


def norm_body(offsets, counts, width, *refs):
    groups = len(offsets)
    gain_ref, out_ref = refs[-2:]
    place = place_on_ring(groups)
    blocks, total, first = [], 0.0, 0
    for count in counts:
        block = sum(ref[...].astype(jnp.float32) for ref in refs[first : first + count])
        total = total + jnp.sum(block * block, axis=1, keepdims=True)
        blocks.append(block)
        first += count
    inverse_rms = lax.rsqrt(total / (groups * width) + 1e-05)
    for offset, block in zip(offsets, blocks):
        q = lax.rem(place + offset + groups, groups)
        d = jnp.where(q < groups // 2, 2 * q, 2 * (groups - 1 - q) + 1)
        columns = pl.ds(pl.multiple_of(d * width, width), width)
        out_ref[:, columns] = (block * inverse_rms * gain_ref[:, columns]).astype(jnp.bfloat16)


VMEM = pl.BlockSpec(memory_space=pltpu.VMEM)


class Gather:
    def __init__(self, own, axis):
        self.ring = ring_of(lax.axis_size("dp"))
        self.axis, self.last, self.hops = axis, len(self.ring) // 2, 0
        self.ends = [own, own]
        self.slots = {0: [own]}

    def hop(self):
        count = len(self.ring)
        ends = self.ends
        self.hops += 1
        if self.hops == self.last:
            middle = ends[0].shape[self.axis] // 2
            ends = [
                lax.slice_in_dim(ends[0], 0, middle, axis=self.axis),
                lax.slice_in_dim(ends[1], middle, 2 * middle, axis=self.axis),
            ]
        up = [(self.ring[q], self.ring[(q + 1) % count]) for q in range(count)]
        down = [(target, source) for source, target in up]
        self.ends = [lax.ppermute(ends[0], "dp", up), lax.ppermute(ends[1], "dp", down)]
        if self.hops == self.last:
            self.slots[self.hops] = self.ends
        else:
            self.slots[self.hops], self.slots[-self.hops] = [self.ends[0]], [self.ends[1]]


def local(attn_heads, residual, low_hidden, mid_hidden, out_weight, join_weight, join_gain):
    groups, owners = lax.axis_size("dp"), lax.axis_size("tensor")
    tokens, features = attn_heads.shape
    width = out_weight.shape[1]
    xs = owners // 2
    rows = tokens // owners
    ring = ring_of(groups)
    last = groups // 2
    offsets = [0] + [sign * s for s in range(1, last) for sign in (1, -1)] + [last]
    tensor = lax.axis_index("tensor").astype(jnp.uint32)
    core, x = tensor & 1, tensor >> 1

    def swap(values, bit):
        return lax.ppermute(values, "tensor", [(t, t ^ bit) for t in range(owners)])

    def product(slots, weight):
        rows_in = jnp.concatenate([piece for slot in slots for piece in slot], axis=0)
        return jnp.dot(rows_in, weight, preferred_element_type=jnp.float32).reshape(len(slots), tokens, width)

    def bit_of_x(half):
        return (x >> (half.bit_length() - 1)) & 1

    attn = Gather(attn_heads, 0)
    per_owner = groups // owners
    classes = list(reversed(range(per_owner)))
    kept = {kind: [k for k in offsets if k % per_owner == kind] for kind in classes}
    kept = {kind: slots[-1:] + slots[:-1] for kind, slots in kept.items()}
    pair_sums = {kind: [None] * xs for kind in classes}

    def multiply_pairs(reach):
        made = {}
        for kind in classes:
            for i in range(xs):
                pair = kept[kind][2 * i : 2 * i + 2]
                if max(abs(k) for k in pair) == reach:
                    made[kind, i] = product([attn.slots[k] for k in pair], out_weight)
        return made

    def sum_cores(made):
        for (kind, i), products in made.items():
            pair_sums[kind][i] = pick(products, core) + swap(pick(products, 1 - core), 1)

    low = Gather(low_hidden, 0)
    mid = Gather(mid_hidden, 0)
    for hop in range(1, last + 1):
        attn.ends, low.ends, mid.ends, pair_sums = tie(attn.ends, low.ends, mid.ends, pair_sums)
        attn.hop()
        (mid if hop == last else low).hop()
        sum_cores(multiply_pairs(hop - 1))
    attn.slots[last], pair_sums = tie(attn.ends, pair_sums)
    sum_cores(multiply_pairs(last))

    def sum_xs(parts):
        while len(parts) > 1:
            half = len(parts) // 2
            high = bit_of_x(half) == 1
            sent = jnp.stack([jnp.where(high, a, b) for a, b in zip(parts[:half], parts[half:])]).astype(jnp.bfloat16)
            came = swap(sent, 2 * half)
            parts = [
                jnp.where(high, b, a) + came[i].astype(jnp.float32)
                for i, (a, b) in enumerate(zip(parts[:half], parts[half:]))
            ]
        return parts[0]

    arrived = []
    for kind in classes:
        held = sum_xs(pair_sums[kind]).astype(jnp.bfloat16)
        if kind == classes[-1]:
            held, mid.ends, low.ends = tie(held, mid.ends, low.ends)
            low.hop()
        moves = [
            (d * owners + t, ring[(p - kept[kind][t]) % groups] * owners + d // per_owner)
            for p, d in enumerate(ring)
            for t in range(owners)
        ]
        arrived.append(lax.ppermute(held, ("dp", "tensor"), moves))
    own_top = pl.pallas_call(
        functools.partial(top_body, groups, classes, width),
        out_shape=jax.ShapeDtypeStruct((tokens, features), jnp.bfloat16),
        in_specs=[VMEM] * (len(classes) + 1),
        out_specs=VMEM,
        name="add_residual",
    )(*arrived, residual)

    own_top, low.slots[last] = tie(own_top, low.slots[last])
    top = Gather(own_top, 0)
    cuts = [0] + list(range(3, groups, 2)) + [groups]
    chunks = [offsets[low_cut:high_cut] for low_cut, high_cut in zip(cuts, cuts[1:])]
    owned = {}

    def multiply_deep(part):
        total = product([low.slots[k] for k in part], join_weight[0])
        return total + product([mid.slots[k] for k in part], join_weight[1])

    def multiply(part, deep_sum):
        return product([top.slots[k] for k in part], join_weight[2]) + deep_sum

    def add_cores(total):
        by_owner = total.reshape(total.shape[0], xs, 2, rows, width)
        kept_part = lax.dynamic_index_in_dim(by_owner, core, 2, keepdims=False)
        sent_part = lax.dynamic_index_in_dim(by_owner, 1 - core, 2, keepdims=False)
        return kept_part + swap(sent_part, 1)

    def send(part, k, flip=0):
        if not k and not flip:
            return part
        moves = [
            (ring[q] * owners + t, ring[(q - k) % groups] * owners + (t ^ (2 * flip)))
            for q in range(groups)
            for t in range(owners)
        ]
        return lax.ppermute(part.astype(jnp.bfloat16), ("dp", "tensor"), moves)

    def add_x(total):
        half = xs // 2
        while half:
            total = total.reshape((total.shape[0], 2, half) + total.shape[-2:])
            side = bit_of_x(half)
            sent = lax.dynamic_index_in_dim(total, 1 - side, 1, keepdims=False).astype(jnp.bfloat16)
            total = lax.dynamic_index_in_dim(total, side, 1, keepdims=False) + swap(sent, 2 * half).astype(jnp.float32)
            half //= 2
        return total.reshape(total.shape[0], rows, width)

    def send_all(part, total):
        for i, k in enumerate(part):
            owned[k] = [send(total[i], k)]

    def add_halves(part, total):
        for flip in range(xs):
            for i, k in enumerate(part):
                owned.setdefault(k, []).append(send(pick(total[i], x ^ flip), k, flip))

    cored, deep_sum, summed = None, None, None
    for hop in range(1, last + 1):
        top.ends, mid.ends, cored, deep_sum = tie(top.ends, mid.ends, cored, deep_sum)
        top.hop()
        if hop != last - 1:
            mid.hop()
        if hop > 2:
            summed = add_x(cored)
            if hop < last:
                send_all(chunks[hop - 3], summed)
        if hop > 1:
            cored = add_cores(multiply(chunks[hop - 2], deep_sum))
        if hop < last:
            deep_sum = multiply_deep(chunks[hop - 1])
    deep_sum = multiply_deep(chunks[-1])
    top.slots[last], owned, summed = tie(top.ends, owned, summed)
    send_all(chunks[-3], summed)
    send_all(chunks[-2], add_x(cored))
    add_halves(chunks[-1], add_cores(multiply(chunks[-1], deep_sum)))
    parts = [part for k in offsets for part in owned[k]]
    counts = [len(owned[k]) for k in offsets]
    return pl.pallas_call(
        functools.partial(norm_body, offsets, counts, width),
        out_shape=jax.ShapeDtypeStruct((rows, groups * width), jnp.bfloat16),
        in_specs=[VMEM] * (len(parts) + 1),
        out_specs=VMEM,
        name="norm_rows",
    )(*parts, join_gain.reshape(1, groups * width))


def solution(mesh):
    return jax.shard_map(
        local,
        mesh=mesh,
        in_specs=(
            P("dp", "tensor"),
            P("dp", "tensor"),
            P("dp", "tensor"),
            P("dp", "tensor"),
            P("tensor", "dp"),
            P(None, "tensor", "dp"),
            P(),
        ),
        out_specs=P(("dp", "tensor"), None),
        check_vma=False,
    )
```

```python
import functools

import jax
import jax.numpy as jnp
from jax import lax
from jax.experimental import pallas as pl
from jax.experimental.pallas import tpu as pltpu
from jax.sharding import PartitionSpec as P


def ring_of(groups):
    half = groups // 2
    return [2 * q for q in range(half)] + [2 * q + 1 for q in reversed(range(half))]


def tie(*values):
    flat, tree = jax.tree.flatten(values)
    return jax.tree.unflatten(tree, lax.optimization_barrier(tuple(flat)))


def pick(values, index):
    return lax.dynamic_index_in_dim(values, index, 0, keepdims=False)


def place_on_ring(groups):
    dp = lax.axis_index("dp")
    return jnp.where(lax.rem(dp, 2) == 0, lax.div(dp, 2), groups - 1 - lax.div(dp, 2))


def top_body(groups, classes, width, *refs):
    arrived, rest_ref, top_ref = refs[: len(classes)], refs[-2], refs[-1]
    home = lax.axis_index("tensor") + place_on_ring(groups)
    for kind, piece_ref in zip(classes, arrived):
        j = lax.rem(home + kind, len(classes))
        columns = pl.ds(pl.multiple_of(j * width, width), width)
        total = rest_ref[:, columns].astype(jnp.float32) + piece_ref[...].astype(jnp.float32)
        top_ref[:, columns] = total.astype(jnp.bfloat16)


def norm_body(offsets, counts, width, *refs):
    groups = len(offsets)
    gain_ref, out_ref = refs[-2:]
    place = place_on_ring(groups)
    blocks, total, first = [], 0.0, 0
    for count in counts:
        block = sum(ref[...].astype(jnp.float32) for ref in refs[first : first + count])
        total = total + jnp.sum(block * block, axis=1, keepdims=True)
        blocks.append(block)
        first += count
    inverse_rms = lax.rsqrt(total / (groups * width) + 1e-05)
    for offset, block in zip(offsets, blocks):
        q = lax.rem(place + offset + groups, groups)
        d = jnp.where(q < groups // 2, 2 * q, 2 * (groups - 1 - q) + 1)
        columns = pl.ds(pl.multiple_of(d * width, width), width)
        out_ref[:, columns] = (block * inverse_rms * gain_ref[:, columns]).astype(jnp.bfloat16)


VMEM = pl.BlockSpec(memory_space=pltpu.VMEM)


class Gather:
    def __init__(self, own, axis):
        self.ring = ring_of(lax.axis_size("dp"))
        self.axis, self.last, self.hops = axis, len(self.ring) // 2, 0
        self.ends = [own, own]
        self.slots = {0: [own]}

    def hop(self):
        count = len(self.ring)
        ends = self.ends
        self.hops += 1
        if self.hops == self.last:
            middle = ends[0].shape[self.axis] // 2
            ends = [
                lax.slice_in_dim(ends[0], 0, middle, axis=self.axis),
                lax.slice_in_dim(ends[1], middle, 2 * middle, axis=self.axis),
            ]
        up = [(self.ring[q], self.ring[(q + 1) % count]) for q in range(count)]
        down = [(target, source) for source, target in up]
        self.ends = [lax.ppermute(ends[0], "dp", up), lax.ppermute(ends[1], "dp", down)]
        if self.hops == self.last:
            self.slots[self.hops] = self.ends
        else:
            self.slots[self.hops], self.slots[-self.hops] = [self.ends[0]], [self.ends[1]]


def local(attn_heads, residual, low_hidden, mid_hidden, out_weight, join_weight, join_gain):
    groups, owners = lax.axis_size("dp"), lax.axis_size("tensor")
    tokens, features = attn_heads.shape
    width = out_weight.shape[1]
    xs = owners // 2
    rows = tokens // owners
    ring = ring_of(groups)
    last = groups // 2
    offsets = [0] + [sign * s for s in range(1, last) for sign in (1, -1)] + [last]
    tensor = lax.axis_index("tensor").astype(jnp.uint32)
    core, x = tensor & 1, tensor >> 1

    def swap(values, bit):
        return lax.ppermute(values, "tensor", [(t, t ^ bit) for t in range(owners)])

    def product(slots, weight):
        rows_in = jnp.concatenate([piece for slot in slots for piece in slot], axis=0)
        return jnp.dot(rows_in, weight, preferred_element_type=jnp.float32).reshape(len(slots), tokens, width)

    def bit_of_x(half):
        return (x >> (half.bit_length() - 1)) & 1

    attn = Gather(attn_heads, 0)
    per_owner = groups // owners
    classes = list(reversed(range(per_owner)))
    kept = {kind: [k for k in offsets if k % per_owner == kind] for kind in classes}
    kept = {kind: slots[-1:] + slots[:-1] for kind, slots in kept.items()}
    pair_sums = {kind: [None] * xs for kind in classes}

    def multiply_pairs(reach):
        made = {}
        for kind in classes:
            for i in range(xs):
                pair = kept[kind][2 * i : 2 * i + 2]
                if max(abs(k) for k in pair) == reach:
                    made[kind, i] = product([attn.slots[k] for k in pair], out_weight)
        return made

    def sum_cores(made):
        for (kind, i), products in made.items():
            pair_sums[kind][i] = pick(products, core) + swap(pick(products, 1 - core), 1)

    low = Gather(low_hidden, 0)
    mid = Gather(mid_hidden, 0)
    for hop in range(1, last + 1):
        attn.ends, low.ends, mid.ends, pair_sums = tie(attn.ends, low.ends, mid.ends, pair_sums)
        attn.hop()
        (mid if hop == last else low).hop()
        sum_cores(multiply_pairs(hop - 1))
    attn.slots[last], pair_sums = tie(attn.ends, pair_sums)
    sum_cores(multiply_pairs(last))

    def sum_xs(parts):
        while len(parts) > 1:
            half = len(parts) // 2
            high = bit_of_x(half) == 1
            sent = jnp.stack([jnp.where(high, a, b) for a, b in zip(parts[:half], parts[half:])]).astype(jnp.bfloat16)
            came = swap(sent, 2 * half)
            parts = [
                jnp.where(high, b, a) + came[i].astype(jnp.float32)
                for i, (a, b) in enumerate(zip(parts[:half], parts[half:]))
            ]
        return parts[0]

    arrived = []
    for kind in classes:
        held = sum_xs(pair_sums[kind]).astype(jnp.bfloat16)
        if kind == classes[-1]:
            held, mid.ends, low.ends = tie(held, mid.ends, low.ends)
            low.hop()
        moves = [
            (d * owners + t, ring[(p - kept[kind][t]) % groups] * owners + d // per_owner)
            for p, d in enumerate(ring)
            for t in range(owners)
        ]
        arrived.append(lax.ppermute(held, ("dp", "tensor"), moves))
    own_top = pl.pallas_call(
        functools.partial(top_body, groups, classes, width),
        out_shape=jax.ShapeDtypeStruct((tokens, features), jnp.bfloat16),
        in_specs=[VMEM] * (len(classes) + 1),
        out_specs=VMEM,
        name="add_residual",
    )(*arrived, residual)

    own_top, low.slots[last] = tie(own_top, low.slots[last])
    top = Gather(own_top, 0)
    cuts = [0] + list(range(3, groups, 2)) + [groups]
    chunks = [offsets[low_cut:high_cut] for low_cut, high_cut in zip(cuts, cuts[1:])]
    owned = {}

    def multiply_deep(part):
        total = product([low.slots[k] for k in part], join_weight[0])
        return total + product([mid.slots[k] for k in part], join_weight[1])

    def multiply(part, deep_sum):
        return product([top.slots[k] for k in part], join_weight[2]) + deep_sum

    def add_cores(total):
        by_owner = total.reshape(total.shape[0], xs, 2, rows, width)
        kept_part = lax.dynamic_index_in_dim(by_owner, core, 2, keepdims=False)
        sent_part = lax.dynamic_index_in_dim(by_owner, 1 - core, 2, keepdims=False)
        return kept_part + swap(sent_part, 1)

    def send(part, k, flip=0):
        if not k and not flip:
            return part
        moves = [
            (ring[q] * owners + t, ring[(q - k) % groups] * owners + (t ^ (2 * flip)))
            for q in range(groups)
            for t in range(owners)
        ]
        return lax.ppermute(part.astype(jnp.bfloat16), ("dp", "tensor"), moves)

    def add_x(total):
        half = xs // 2
        while half:
            total = total.reshape((total.shape[0], 2, half) + total.shape[-2:])
            side = bit_of_x(half)
            sent = lax.dynamic_index_in_dim(total, 1 - side, 1, keepdims=False).astype(jnp.bfloat16)
            total = lax.dynamic_index_in_dim(total, side, 1, keepdims=False) + swap(sent, 2 * half).astype(jnp.float32)
            half //= 2
        return total.reshape(total.shape[0], rows, width)

    def send_all(part, total):
        for i, k in enumerate(part):
            owned[k] = [send(total[i], k)]

    def add_halves(part, total):
        for flip in range(xs):
            for i, k in enumerate(part):
                owned.setdefault(k, []).append(send(pick(total[i], x ^ flip), k, flip))

    cored, deep_sum, summed = None, None, None
    for hop in range(1, last + 1):
        top.ends, mid.ends, cored, deep_sum, summed = tie(top.ends, mid.ends, cored, deep_sum, summed)
        top.hop()
        if hop != last - 1:
            mid.hop()
        if hop > 3:
            send_all(chunks[hop - 4], summed)
        if hop > 2:
            summed = add_x(cored)
        if hop > 1:
            cored = add_cores(multiply(chunks[hop - 2], deep_sum))
        if hop < last:
            deep_sum = multiply_deep(chunks[hop - 1])
    deep_sum = multiply_deep(chunks[-1])
    top.slots[last], summed = tie(top.ends, summed)
    send_all(chunks[-3], summed)
    send_all(chunks[-2], add_x(cored))
    add_halves(chunks[-1], add_cores(multiply(chunks[-1], deep_sum)))
    parts = [part for k in offsets for part in owned[k]]
    counts = [len(owned[k]) for k in offsets]
    return pl.pallas_call(
        functools.partial(norm_body, offsets, counts, width),
        out_shape=jax.ShapeDtypeStruct((rows, groups * width), jnp.bfloat16),
        in_specs=[VMEM] * (len(parts) + 1),
        out_specs=VMEM,
        name="norm_rows",
    )(*parts, join_gain.reshape(1, groups * width))


def solution(mesh):
    return jax.shard_map(
        local,
        mesh=mesh,
        in_specs=(
            P("dp", "tensor"),
            P("dp", "tensor"),
            P("dp", "tensor"),
            P("dp", "tensor"),
            P("tensor", "dp"),
            P(None, "tensor", "dp"),
            P(),
        ),
        out_specs=P(("dp", "tensor"), None),
        check_vma=False,
    )
```

```python
import functools

import jax
import jax.numpy as jnp
from jax import lax
from jax.experimental import pallas as pl
from jax.experimental.pallas import tpu as pltpu
from jax.sharding import PartitionSpec as P


def ring_of(groups):
    half = groups // 2
    return [2 * q for q in range(half)] + [2 * q + 1 for q in reversed(range(half))]


def tie(*values):
    flat, tree = jax.tree.flatten(values)
    return jax.tree.unflatten(tree, lax.optimization_barrier(tuple(flat)))


def pick(values, index):
    return lax.dynamic_index_in_dim(values, index, 0, keepdims=False)


def place_on_ring(groups):
    dp = lax.axis_index("dp")
    return jnp.where(lax.rem(dp, 2) == 0, lax.div(dp, 2), groups - 1 - lax.div(dp, 2))


def top_body(groups, classes, width, *refs):
    arrived, rest_ref, top_ref = refs[: len(classes)], refs[-2], refs[-1]
    home = lax.axis_index("tensor") + place_on_ring(groups)
    for kind, piece_ref in zip(classes, arrived):
        j = lax.rem(home + kind, len(classes))
        columns = pl.ds(pl.multiple_of(j * width, width), width)
        total = rest_ref[:, columns].astype(jnp.float32) + piece_ref[...].astype(jnp.float32)
        top_ref[:, columns] = total.astype(jnp.bfloat16)


def norm_body(offsets, counts, width, *refs):
    groups = len(offsets)
    gain_ref, out_ref = refs[-2:]
    place = place_on_ring(groups)
    blocks, total, first = [], 0.0, 0
    for count in counts:
        block = sum(ref[...].astype(jnp.float32) for ref in refs[first : first + count])
        total = total + jnp.sum(block * block, axis=1, keepdims=True)
        blocks.append(block)
        first += count
    inverse_rms = lax.rsqrt(total / (groups * width) + 1e-05)
    for offset, block in zip(offsets, blocks):
        q = lax.rem(place + offset + groups, groups)
        d = jnp.where(q < groups // 2, 2 * q, 2 * (groups - 1 - q) + 1)
        columns = pl.ds(pl.multiple_of(d * width, width), width)
        out_ref[:, columns] = (block * inverse_rms * gain_ref[:, columns]).astype(jnp.bfloat16)


VMEM = pl.BlockSpec(memory_space=pltpu.VMEM)


class Gather:
    def __init__(self, own, axis):
        self.ring = ring_of(lax.axis_size("dp"))
        self.axis, self.last, self.hops = axis, len(self.ring) // 2, 0
        self.ends = [own, own]
        self.slots = {0: [own]}

    def hop(self):
        count = len(self.ring)
        ends = self.ends
        self.hops += 1
        if self.hops == self.last:
            middle = ends[0].shape[self.axis] // 2
            ends = [
                lax.slice_in_dim(ends[0], 0, middle, axis=self.axis),
                lax.slice_in_dim(ends[1], middle, 2 * middle, axis=self.axis),
            ]
        up = [(self.ring[q], self.ring[(q + 1) % count]) for q in range(count)]
        down = [(target, source) for source, target in up]
        self.ends = [lax.ppermute(ends[0], "dp", up), lax.ppermute(ends[1], "dp", down)]
        if self.hops == self.last:
            self.slots[self.hops] = self.ends
        else:
            self.slots[self.hops], self.slots[-self.hops] = [self.ends[0]], [self.ends[1]]


def local(attn_heads, residual, low_hidden, mid_hidden, out_weight, join_weight, join_gain):
    groups, owners = lax.axis_size("dp"), lax.axis_size("tensor")
    tokens, features = attn_heads.shape
    width = out_weight.shape[1]
    xs = owners // 2
    rows = tokens // owners
    ring = ring_of(groups)
    last = groups // 2
    offsets = [0] + [sign * s for s in range(1, last) for sign in (1, -1)] + [last]
    tensor = lax.axis_index("tensor").astype(jnp.uint32)
    core, x = tensor & 1, tensor >> 1

    def swap(values, bit):
        return lax.ppermute(values, "tensor", [(t, t ^ bit) for t in range(owners)])

    def product(slots, weight):
        rows_in = jnp.concatenate([piece for slot in slots for piece in slot], axis=0)
        return jnp.dot(rows_in, weight, preferred_element_type=jnp.float32).reshape(len(slots), tokens, width)

    def bit_of_x(half):
        return (x >> (half.bit_length() - 1)) & 1

    attn = Gather(attn_heads, 0)
    per_owner = groups // owners
    classes = list(reversed(range(per_owner)))
    kept = {kind: [k for k in offsets if k % per_owner == kind] for kind in classes}
    kept = {kind: slots[-1:] + slots[:-1] for kind, slots in kept.items()}
    pair_sums = {kind: [None] * xs for kind in classes}

    def multiply_pairs(reach):
        made = {}
        for kind in classes:
            for i in range(xs):
                pair = kept[kind][2 * i : 2 * i + 2]
                if max(abs(k) for k in pair) == reach:
                    made[kind, i] = product([attn.slots[k] for k in pair], out_weight)
        return made

    def sum_cores(made):
        for (kind, i), products in made.items():
            pair_sums[kind][i] = pick(products, core) + swap(pick(products, 1 - core), 1)

    low = Gather(low_hidden, 0)
    mid = Gather(mid_hidden, 0)
    made = {}
    for hop in range(1, last + 1):
        attn.ends, low.ends, mid.ends, values = tie(attn.ends, low.ends, mid.ends, list(made.values()))
        made = dict(zip(made, values))
        attn.hop()
        (mid if hop == last else low).hop()
        sum_cores(made)
        made = multiply_pairs(hop - 1)
    low.ends, attn.ends = tie(low.ends, attn.ends)
    low.hop()
    sum_cores(made)
    attn.slots[last], pair_sums = tie(attn.ends, pair_sums)
    sum_cores(multiply_pairs(last))

    def sum_xs(parts):
        while len(parts) > 1:
            half = len(parts) // 2
            high = bit_of_x(half) == 1
            sent = jnp.stack([jnp.where(high, a, b) for a, b in zip(parts[:half], parts[half:])]).astype(jnp.bfloat16)
            came = swap(sent, 2 * half)
            parts = [
                jnp.where(high, b, a) + came[i].astype(jnp.float32)
                for i, (a, b) in enumerate(zip(parts[:half], parts[half:]))
            ]
        return parts[0]

    arrived = []
    for kind in classes:
        held, mid.ends = tie(sum_xs(pair_sums[kind]).astype(jnp.bfloat16), mid.ends)
        moves = [
            (d * owners + t, ring[(p - kept[kind][t]) % groups] * owners + d // per_owner)
            for p, d in enumerate(ring)
            for t in range(owners)
        ]
        arrived.append(lax.ppermute(held, ("dp", "tensor"), moves))
    own_top = pl.pallas_call(
        functools.partial(top_body, groups, classes, width),
        out_shape=jax.ShapeDtypeStruct((tokens, features), jnp.bfloat16),
        in_specs=[VMEM] * (len(classes) + 1),
        out_specs=VMEM,
        name="add_residual",
    )(*arrived, residual)

    own_top, low.slots[last] = tie(own_top, low.slots[last])
    top = Gather(own_top, 0)
    cuts = [0] + list(range(3, groups, 2)) + [groups]
    chunks = [offsets[low_cut:high_cut] for low_cut, high_cut in zip(cuts, cuts[1:])]
    owned = {}

    def multiply_deep(part):
        total = product([low.slots[k] for k in part], join_weight[0])
        return total + product([mid.slots[k] for k in part], join_weight[1])

    def multiply(part, deep_sum):
        return product([top.slots[k] for k in part], join_weight[2]) + deep_sum

    def add_cores(total):
        by_owner = total.reshape(total.shape[0], xs, 2, rows, width)
        kept_part = lax.dynamic_index_in_dim(by_owner, core, 2, keepdims=False)
        sent_part = lax.dynamic_index_in_dim(by_owner, 1 - core, 2, keepdims=False)
        return kept_part + swap(sent_part, 1)

    def send(part, k, flip=0):
        if not k and not flip:
            return part
        moves = [
            (ring[q] * owners + t, ring[(q - k) % groups] * owners + (t ^ (2 * flip)))
            for q in range(groups)
            for t in range(owners)
        ]
        return lax.ppermute(part.astype(jnp.bfloat16), ("dp", "tensor"), moves)

    def add_x(part, total, dtype):
        half = xs // 2
        while half:
            total = total.reshape((total.shape[0], 2, half) + total.shape[-2:])
            side = bit_of_x(half)
            sent = lax.dynamic_index_in_dim(total, 1 - side, 1, keepdims=False).astype(dtype)
            total = lax.dynamic_index_in_dim(total, side, 1, keepdims=False) + swap(sent, 2 * half).astype(jnp.float32)
            half //= 2
        total = total.reshape(total.shape[0], rows, width)
        for i, k in enumerate(part):
            owned[k] = [send(total[i], k)]

    def add_halves(part, total):
        for flip in range(xs):
            for i, k in enumerate(part):
                owned.setdefault(k, []).append(send(pick(total[i], x ^ flip), k, flip))

    cored, deep_sum = {}, None
    for hop in range(1, last + 1):
        top.ends, mid.ends, cored, deep_sum = tie(top.ends, mid.ends, cored, deep_sum)
        top.hop()
        if mid.hops < last:
            mid.hop()
        for n, total in cored.items():
            add_x(chunks[n], total, jnp.float32 if n == 0 else jnp.bfloat16)
        cored = {hop - 2: add_cores(multiply(chunks[hop - 2], deep_sum))} if hop > 1 else {}
        deep_sum = multiply_deep(chunks[hop - 1])
    for n, total in cored.items():
        add_x(chunks[n], total, jnp.bfloat16)
    early = {k: owned[k] for part in chunks[:-3] for k in part}
    top.slots[last], early, deep_sum = tie(top.ends, early, deep_sum)
    owned.update(early)
    add_halves(chunks[-1], add_cores(multiply(chunks[-1], deep_sum)))
    parts = [part for k in offsets for part in owned[k]]
    counts = [len(owned[k]) for k in offsets]
    return pl.pallas_call(
        functools.partial(norm_body, offsets, counts, width),
        out_shape=jax.ShapeDtypeStruct((rows, groups * width), jnp.bfloat16),
        in_specs=[VMEM] * (len(parts) + 1),
        out_specs=VMEM,
        name="norm_rows",
    )(*parts, join_gain.reshape(1, groups * width))


def solution(mesh):
    return jax.shard_map(
        local,
        mesh=mesh,
        in_specs=(
            P("dp", "tensor"),
            P("dp", "tensor"),
            P("dp", "tensor"),
            P("dp", "tensor"),
            P("tensor", "dp"),
            P(None, "tensor", "dp"),
            P(),
        ),
        out_specs=P(("dp", "tensor"), None),
        check_vma=False,
    )
```
